32 devices in a mesh: row: 4 (over y, x), col: 4 (over z), dp: 2 (over core).
Axes of the slice: x: 2, y: 2, z: 4, core: 2. Of those that a mesh axis runs over, the one named last changes fastest.
Arguments:
- grad_output: bfloat16 [2, 512, 8192], P('dp', 'col', 'row'), may hold values from -0.09375 to 0.09375
- block_input: bfloat16 [2, 512, 8192], P('dp', 'col', 'row'), may hold values from -6 to 6
- query_branch: bfloat16 [2, 512, 8192], P('dp', 'row', 'col'), may hold values from -6 to 6
- key_branch: bfloat16 [2, 512, 8192], P('dp', 'row', 'col'), may hold values from -6 to 6
- value_branch: bfloat16 [2, 512, 8192], P('dp', 'row', 'col'), may hold values from -6 to 6
- out_weight: bfloat16 [8192, 8192], P('row', 'col'), may hold values from -0.0625 to 0.0625
- filters: float32 [512, 128], P('col'), may hold values from -0.5 to 0.5
Outputs:
- out_weight_grad: float32 [8192, 8192], P('row', 'col')
- value_weight_grad: float32 [8192, 8192], P('col', 'row')
- filter_grad: float32 [512, 128], P('col')
The draws below stay inside these ranges and needn't reach their ends.
All inputs are finite; a program needn't handle non-finite values.
Results may differ from the reference program's by a relative error of at most 0.0029.
Values may be sent and summed in bfloat16 or wider, within the bound.
No kernel may reach another device: no remote copies, remote signals or barrier semaphores. Data moves between devices by JAX's collectives and lax.ppermute only.
A program may use at most 128 MiB of HBM per device.

```python
import jax
import jax.numpy as jnp
from jax import lax

D = 8192
GROUPS = 512
KLEN = 128
TOKENS = 512
SEQS = 2


def steps_of(own_key, shape, pieces, least, high):
    factor_of, own = 1.0, jax.random.fold_in(own_key, 6)
    for dim, parts in pieces:
        steps = jnp.exp(jax.random.uniform(jax.random.fold_in(own, dim), (parts,), jnp.float32, least / len(pieces), high / len(pieces)))
        factor_of = factor_of * jnp.repeat(steps, shape[dim] // parts).reshape([-1 if axis == dim else 1 for axis in range(len(shape))])
    return factor_of


def noise(own_key, shape, scale, most, shards=(), held_as=jnp.bfloat16):
    result = jax.random.normal(own_key, shape, jnp.float32) * scale
    if len(shards) > 0:
        result = steps_of(own_key, shape, shards, -0.22, 0.18) * result
    return jnp.clip(result, min=-most, max=most).astype(held_as)


def setup_inputs(seed: int = 0) -> dict:
    key_list = jax.random.split(jax.random.key(seed), 8)
    grad_output = noise(key_list[0], (SEQS, TOKENS, D), 0.015625, 0.09375, ((0, 2), (1, 4), (2, 4)))
    block_input = noise(key_list[1], (SEQS, TOKENS, D), 1.0, 6.0, ((0, 2), (1, 4), (2, 4)))
    query_branch = noise(key_list[2], (SEQS, TOKENS, D), 1.0, 6.0, ((0, 2), (1, 4), (2, 4)))
    key_branch = noise(key_list[3], (SEQS, TOKENS, D), 1.0, 6.0, ((0, 2), (1, 4), (2, 4)))
    value_branch = noise(key_list[4], (SEQS, TOKENS, D), 1.0, 6.0, ((0, 2), (1, 4), (2, 4)))
    out_weight = noise(key_list[5], (D, D), D ** -0.5, 0.0625, ((0, 4), (1, 4)))
    filters = noise(key_list[6], (GROUPS, KLEN), 0.09, 0.5, ((0, 4),), jnp.float32)
    return dict(grad_output=grad_output, block_input=block_input, query_branch=query_branch, key_branch=key_branch, value_branch=value_branch, out_weight=out_weight, filters=filters)


highest = lax.Precision.HIGHEST

def causal_mix(signal, per_channel):
    seqs, length, width = signal.shape
    lag_count = per_channel.shape[1]
    padded = jnp.pad(signal, ((0, 0), (lag_count, 0), (0, 0)))
    anchor = jnp.zeros((), jnp.int32)

    def add_lag(lag, total):
        shift_at = (lag_count - lag).astype(jnp.int32)
        moved = lax.dynamic_slice(padded, (anchor, shift_at, anchor), (seqs, length, width))
        column = lax.dynamic_index_in_dim(per_channel, lag.astype(jnp.int32), 1, keepdims=False)
        return total + column * moved
    return lax.fori_loop(0, lag_count, add_lag, jnp.zeros(signal.shape, jnp.float32))

def later_mix(signal, per_channel):
    seqs, length, width = signal.shape
    lag_count = per_channel.shape[1]
    padded = jnp.pad(signal, ((0, 0), (0, lag_count), (0, 0)))
    anchor = jnp.zeros((), jnp.int32)

    def add_lag(lag, total):
        moved = lax.dynamic_slice(padded, (anchor, lag.astype(jnp.int32), anchor), (seqs, length, width))
        column = lax.dynamic_index_in_dim(per_channel, lag.astype(jnp.int32), 1, keepdims=False)
        return total + column * moved
    return lax.fori_loop(0, lag_count, add_lag, jnp.zeros(signal.shape, jnp.float32))

def taps_grad(delta_mix, mixed, group_size):
    seqs, length, width = mixed.shape
    padded = jnp.pad(mixed, ((0, 0), (KLEN, 0), (0, 0)))
    anchor = jnp.zeros((), jnp.int32)

    def one_lag(lag):
        shift_at = (KLEN - lag).astype(jnp.int32)
        moved = lax.dynamic_slice(padded, (anchor, shift_at, anchor), (seqs, length, width))
        per_chan = lax.optimization_barrier(jnp.sum(delta_mix * moved, axis=(0, 1)))
        return lax.optimization_barrier(jnp.sum(per_chan.reshape(-1, group_size), axis=1))
    return lax.map(one_lag, jnp.arange(KLEN, dtype=jnp.int32)).T

def reference(grad_output, block_input, query_branch, key_branch, value_branch, out_weight, filters):
    group_size = D // GROUPS
    per_channel = jnp.repeat(filters, group_size, axis=0)
    mixed = key_branch.astype(jnp.float32) * value_branch.astype(jnp.float32)
    conv_out = causal_mix(mixed, per_channel)
    gated = (query_branch.astype(jnp.float32) * conv_out).astype(jnp.bfloat16)
    flat_grad = grad_output.reshape(-1, D)
    delta_out = jnp.dot(flat_grad, out_weight, preferred_element_type=jnp.float32).reshape(query_branch.shape)
    delta_mix = delta_out * query_branch.astype(jnp.float32)
    delta_conv = later_mix(delta_mix, per_channel)
    delta_value = (delta_conv * key_branch.astype(jnp.float32)).astype(jnp.bfloat16)
    filter_grad = taps_grad(delta_mix, mixed, group_size)
    out_weight_grad = jnp.dot(flat_grad.T, gated.reshape(-1, D), preferred_element_type=jnp.float32)
    value_weight_grad = jnp.dot(delta_value.reshape(-1, D).T, block_input.reshape(-1, D), preferred_element_type=jnp.float32)
    return (out_weight_grad, value_weight_grad, filter_grad)
```

```python
import functools

import jax
import jax.numpy as jnp
from jax import lax
from jax.experimental import pallas as pl
from jax.experimental.pallas import tpu as pltpu
from jax.sharding import PartitionSpec as P

highest = lax.Precision.HIGHEST
f32, bf16 = jnp.float32, jnp.bfloat16
MIB = 1 << 20
VMEM = pl.BlockSpec(memory_space=pltpu.VMEM)
SMEM = pl.BlockSpec(memory_space=pltpu.SMEM)
ANY = pl.BlockSpec(memory_space=pl.ANY)


def params(mib):
    return pltpu.CompilerParams(vmem_limit_bytes=mib * MIB)


def cost(flops, nbytes):
    return pl.CostEstimate(flops=int(flops), bytes_accessed=int(nbytes), transcendentals=0)


def split_two(x):
    hi = x.astype(bf16)
    return hi, (x - hi.astype(f32)).astype(bf16)


def turn_kernel(rows, pos_ref, q_ref, k_ref, v_ref, *outs):
    width = outs[0].shape[1]
    for j, out in enumerate(outs):
        columns = pl.ds(pl.multiple_of((pos_ref[0] ^ j) * width, 128), width)
        for n, src in enumerate((q_ref, k_ref, v_ref)):
            out[n] = src[0, :, columns].T


def turn_branches(pos, q, k, v, rows):
    _, toks, channels = q.shape
    width = channels // rows
    out = jax.ShapeDtypeStruct((3, width, toks), bf16)
    return pl.pallas_call(
        functools.partial(turn_kernel, rows),
        out_shape=[out] * rows,
        in_specs=[SMEM] + [VMEM] * 3,
        out_specs=[VMEM] * rows,
        compiler_params=params(32),
        cost_estimate=cost(0, 4 * q.size * 3),
    )(pos, q, k, v)


def tap_matrix(f_ref, row):
    taps = f_ref.shape[1]
    wide = jnp.broadcast_to(f_ref[pl.ds(row, 1), :], (taps, taps))
    ring = pltpu.roll(wide, 0, 1, stride=1, stride_axis=0)
    s = lax.broadcasted_iota(jnp.int32, (taps, taps), 0)
    t = lax.broadcasted_iota(jnp.int32, (taps, taps), 1)
    same = jnp.where(t >= s, ring, 0.0)
    return same, ring - same


def dot(a, b, dims=((1,), (0,))):
    return lax.dot_general(a, b, (dims, ((), ())), preferred_element_type=f32)


def forward_kernel(size, pos_ref, f_ref, b0, b1, b2, b3, out_ref, mh, ml, qs, gt):
    n = f_ref.shape[1]
    width, toks = gt.shape
    blocks = toks // n
    groups = width // size
    mh[:, :n] = jnp.zeros((width, n), bf16)
    ml[:, :n] = jnp.zeros((width, n), bf16)
    for j, b in enumerate((b0, b1, b2, b3)):
        place = pl.multiple_of((pos_ref[0] ^ j) * n, n)
        hi, lo = split_two(b[1].astype(f32) * b[2].astype(f32))
        mh[:, pl.ds(place + n, n)] = hi
        ml[:, pl.ds(place + n, n)] = lo
        qs[:, pl.ds(place, n)] = b[0]

    def one(g, carry):
        rows = pl.ds(pl.multiple_of(g * size, size), size)
        same, prev = tap_matrix(f_ref, pos_ref[0] * groups + g)
        table_hi, table_lo = split_two(jnp.concatenate([prev, same], axis=0))
        x_hi = jnp.concatenate([mh[rows, b * n : (b + 2) * n] for b in range(blocks)], axis=0)
        x_lo = jnp.concatenate([ml[rows, b * n : (b + 2) * n] for b in range(blocks)], axis=0)
        conv = dot(x_hi, table_hi) + dot(x_lo, table_hi) + dot(x_hi, table_lo)
        for b in range(blocks):
            gate = qs[rows, b * n : (b + 1) * n].astype(f32)
            gt[rows, b * n : (b + 1) * n] = gate * conv[b * size : (b + 1) * size]
        return carry

    lax.fori_loop(0, groups, one, 0, unroll=4)
    for b in range(blocks):
        out_ref[b * n : (b + 1) * n, :] = gt[:, b * n : (b + 1) * n].T.astype(bf16)


def forward(pos, filters, parts, size):
    _, width, n = parts[0].shape
    toks = n * len(parts)
    return pl.pallas_call(
        functools.partial(forward_kernel, size),
        out_shape=jax.ShapeDtypeStruct((toks, width), bf16),
        in_specs=[SMEM] + [VMEM] * 5,
        out_specs=VMEM,
        scratch_shapes=[
            pltpu.VMEM((width, toks + n), bf16),
            pltpu.VMEM((width, toks + n), bf16),
            pltpu.VMEM((width, toks), bf16),
            pltpu.VMEM((width, toks), f32),
        ],
        compiler_params=params(32),
        cost_estimate=cost(8e9, 2 * 4 * toks * width),
    )(pos, filters, *parts)


def backward_kernel(size, counts, pos_ref, f_ref, b0, b1, b2, b3, *refs):
    n = f_ref.shape[1]
    deltas, (taps_ref, out_ref), (dh, dl, mh, ml, qs, ks, sums) = (
        refs[: -9],
        refs[-9:-7],
        refs[-7:],
    )
    width, toks = qs.shape
    blocks = toks // n
    groups = width // size
    row, col = pos_ref[0], pos_ref[1]
    zero = jnp.zeros((width, n), bf16)
    mh[:, :n] = zero
    ml[:, :n] = zero
    dh[:, toks:] = zero
    dl[:, toks:] = zero
    for j, b in enumerate((b0, b1, b2, b3)):
        place = pl.multiple_of((row ^ j) * n, n)
        hi, lo = split_two(b[1].astype(f32) * b[2].astype(f32))
        mh[:, pl.ds(place + n, n)] = hi
        ml[:, pl.ds(place + n, n)] = lo
        qs[:, pl.ds(place, n)] = b[0]
        ks[:, pl.ds(place, n)] = b[1]
    slot = 0
    for i, count in enumerate(counts):
        for m in range(count):
            place = pl.multiple_of((col ^ slot) * n, n)
            own, first, second, third = (ref[m * n : (m + 1) * n, :].astype(f32) for ref in deltas[4 * i : 4 * i + 4])
            delta = (own + first) + (second + third)
            hi, lo = split_two(delta.T * qs[:, pl.ds(place, n)].astype(f32))
            dh[:, pl.ds(place, n)] = hi
            dl[:, pl.ds(place, n)] = lo
            slot += 1
    s = lax.broadcasted_iota(jnp.int32, (n, n), 0)
    t = lax.broadcasted_iota(jnp.int32, (n, n), 1)

    def one(g, carry):
        rows = pl.ds(pl.multiple_of(g * size, size), size)
        same, prev = tap_matrix(f_ref, row * groups + g)
        table_hi, table_lo = split_two(jnp.concatenate([same, prev], axis=1))
        d_hi = [dh[rows, b * n : (b + 2) * n] for b in range(blocks)]
        d_lo = [dl[rows, b * n : (b + 2) * n] for b in range(blocks)]
        x_hi, x_lo = jnp.concatenate(d_hi, axis=0), jnp.concatenate(d_lo, axis=0)
        across = ((1,), (1,))
        conv = dot(x_hi, table_hi, across) + dot(x_lo, table_hi, across) + dot(x_hi, table_lo, across)
        for b in range(blocks):
            key = ks[rows, b * n : (b + 1) * n].astype(f32)
            out_ref[rows, b * n : (b + 1) * n] = (key * conv[b * size : (b + 1) * size]).astype(bf16)
        m_hi = [mh[rows, b * n : (b + 2) * n] for b in range(blocks)]
        m_lo = [ml[rows, b * n : (b + 2) * n] for b in range(blocks)]
        d_hi, d_lo = [d[:, :n] for d in d_hi], [d[:, :n] for d in d_lo]
        pairs = dot(
            jnp.concatenate(m_hi + m_lo + m_hi, axis=0),
            jnp.concatenate(d_hi + d_hi + d_lo, axis=0),
            ((0,), (0,)),
        )
        ring = jnp.where(s <= t, pairs[n:], pairs[:n])
        half = n // 2
        while half >= 8:
            ring = ring[:half] + pltpu.roll(ring[half:], n - half, 1)
            half //= 2
        sums[pl.ds(pl.multiple_of(g * 8, 8), 8), :] = ring
        return carry

    lax.fori_loop(0, groups, one, 0, unroll=4)
    total = sums[pl.ds(0, groups, stride=8), :]
    for i in range(1, 8):
        total = total + pltpu.roll(sums[pl.ds(i, groups, stride=8), :], n - i, 1)
    taps_ref[...] = total


def backward(pos, filters, parts, deltas, counts, size):
    _, width, n = parts[0].shape
    toks = n * len(parts)
    groups = width // size
    return pl.pallas_call(
        functools.partial(backward_kernel, size, counts),
        out_shape=[
            jax.ShapeDtypeStruct((groups, n), f32),
            jax.ShapeDtypeStruct((width, toks), bf16),
        ],
        in_specs=[SMEM] + [VMEM] * (5 + len(deltas)),
        out_specs=[VMEM] * 2,
        scratch_shapes=[pltpu.VMEM((width, toks + n), bf16)] * 4
        + [pltpu.VMEM((width, toks), bf16)] * 2
        + [pltpu.VMEM((8 * groups, n), f32)],
        compiler_params=params(40),
        cost_estimate=cost(8e9, 2 * 8 * toks * width),
    )(pos, filters, *parts, *deltas)


def project_kernel(count, pos_ref, *refs):
    slots, w_ref, outs = refs[:count], refs[count], refs[count + 1 : count + 5]
    wide, sem = refs[count + 5 :]
    width = outs[0].shape[1]
    n = slots[0].shape[0]

    def fetch(j):
        columns = pl.ds(pl.multiple_of((pos_ref[0] ^ j) * width, 128), width)
        return pltpu.make_async_copy(w_ref.at[:, columns], wide.at[j], sem.at[j])

    order = (3, 1, 2, 0)
    for j in order:
        fetch(j).start()
    grads = jnp.concatenate([slot[...] for slot in slots], axis=0)
    for j in order:
        fetch(j).wait()
        outs[j][...] = dot(grads, wide[j]).astype(outs[j].dtype)


def project(pos, slots, weight, rows):
    depth, channels = weight.shape
    width = channels // rows
    toks = sum(slot.shape[0] for slot in slots)
    return pl.pallas_call(
        functools.partial(project_kernel, len(slots)),
        out_shape=[jax.ShapeDtypeStruct((toks, width), f32 if j == 0 else bf16) for j in range(rows)],
        in_specs=[SMEM] + [VMEM] * len(slots) + [ANY],
        out_specs=[VMEM] * rows,
        scratch_shapes=[pltpu.VMEM((rows, depth, width), bf16), pltpu.SemaphoreType.DMA((rows,))],
        compiler_params=params(40),
        cost_estimate=cost(2 * toks * depth * channels, 2 * weight.size),
    )(pos, *slots, weight)


def gradient_kernel(turned, pos_ref, *refs):
    (out_ref, left, right, buf, sem_in, sem_out) = refs[-6:]
    sources = refs[:-6]
    n = 128
    row, col, dp = pos_ref[0], pos_ref[1], pos_ref[2]
    copies = []

    def fetch(src, dst):
        copies.append(pltpu.make_async_copy(src, dst, sem_in.at[len(copies)]))

    seq = left.shape[0] // 2 if turned else left.shape[1] // 2
    if turned:
        slots, gathered = sources[:8], sources[8]
        for i, slot in enumerate(slots):
            owner = dp if i < 4 else 1 - dp
            fetch(slot, left.at[pl.ds(pl.multiple_of(owner * seq + (col ^ (i % 4)) * n, n), n), :])
        width = gathered.shape[2]
        for i in range(8):
            fetch(gathered.at[i], right.at[pl.ds((i % 2) * seq, seq), pl.ds((i // 2) * width, width)])
    else:
        slots, pieces = sources[:8], sources[8:]
        for i, slot in enumerate(slots):
            place = pl.multiple_of((i // 4) * seq + (col ^ (i % 4)) * n, n)
            fetch(slot, right.at[pl.ds(place, n), :])
        width = pieces[0].shape[0]
        for i, piece in enumerate(pieces):
            place = pl.multiple_of((row ^ (i % 4)) * width, width)
            fetch(piece, left.at[pl.ds(place, width), pl.ds((i // 4) * seq, seq)])
    for copy in copies:
        copy.start()
    for copy in copies:
        copy.wait()
    tile = buf.shape[1]
    tiles = out_ref.shape[0] // tile

    def send(i):
        at = pl.ds(pl.multiple_of(i * tile, tile), tile)
        return pltpu.make_async_copy(buf.at[i % 2], out_ref.at[at, :], sem_out.at[i % 2])

    def one(i, carry):
        at = pl.ds(pl.multiple_of(i * tile, tile), tile)

        @pl.when(i >= 2)
        def _():
            send(i - 2).wait()

        lhs = left[:, at].T if turned else left[at, :]
        buf[i % 2] = dot(lhs, right[...])
        send(i).start()
        return carry

    lax.fori_loop(0, tiles, one, 0)
    send(tiles - 2).wait()
    send(tiles - 1).wait()


def gradient(pos, sources, toks, left_width, right_width, turned):
    tile = 256
    return pl.pallas_call(
        functools.partial(gradient_kernel, turned),
        out_shape=jax.ShapeDtypeStruct((left_width, right_width), f32),
        in_specs=[SMEM] + [ANY] * len(sources),
        out_specs=ANY,
        scratch_shapes=[
            pltpu.VMEM((toks, left_width) if turned else (left_width, toks), bf16),
            pltpu.VMEM((toks, right_width), bf16),
            pltpu.VMEM((2, tile, right_width), f32),
            pltpu.SemaphoreType.DMA((16,)),
            pltpu.SemaphoreType.DMA((2,)),
        ],
        compiler_params=params(48),
        cost_estimate=cost(2 * toks * left_width * right_width, 4 * left_width * right_width),
    )(pos, *sources)


near = [(0, 1), (1, 0), (2, 3), (3, 2)]
far = [(0, 2), (2, 0), (1, 3), (3, 1)]
across = [(0, 3), (3, 0), (1, 2), (2, 1)]
swap = [(0, 1), (1, 0)]


def line_slots(x):
    c = lax.axis_index("col")
    first = lax.ppermute(x, "col", near)
    second = lax.ppermute(x, "col", far)
    inner = lax.ppermute(x, "col", [(1, 2), (2, 1)])
    passed = lax.ppermute(second, "col", [(2, 3), (1, 0)])
    third = jnp.where((c == 1) | (c == 2), inner, passed)
    return [x, first, second, third]


def row_exchange(pieces):
    return [
        pieces[0],
        lax.ppermute(pieces[1], "row", near),
        lax.ppermute(pieces[2], "row", far),
        lax.ppermute(pieces[3], "row", across),
    ]


def other_core(xs):
    return [lax.ppermute(x, "dp", swap) for x in xs]


def local(grad_output, block_input, query_branch, key_branch, value_branch, out_weight, filters):
    rows = lax.axis_size("row")
    toks = query_branch.shape[1]
    channels = query_branch.shape[2]
    size = channels // filters.shape[0]
    width = channels // rows
    local_groups = width // size
    pos = jnp.stack([lax.axis_index("row"), lax.axis_index("col"), lax.axis_index("dp")]).astype(jnp.int32)

    grads = line_slots(grad_output[0])
    turned = turn_branches(pos, query_branch, key_branch, value_branch, rows)
    parts = row_exchange(turned)
    gated = forward(pos, filters, parts, size)
    gated_all = lax.all_gather(gated, ("row", "dp"), axis=0)
    inputs = line_slots(block_input[0])

    counts = (3, 1)
    deltas = []
    for chosen in (grads[:3], grads[3:]):
        deltas += row_exchange(project(pos, chosen, out_weight, rows))
    taps, value_grad = backward(pos, filters, parts, deltas, counts, size)
    values = row_exchange([value_grad] * 4)

    out_grad = gradient(
        pos, grads + other_core(grads) + [gated_all], 2 * rows * toks, grad_output.shape[2], channels, True
    )
    weight_grad = gradient(
        pos,
        inputs + other_core(inputs) + values + other_core(values),
        2 * rows * toks,
        channels,
        block_input.shape[2],
        False,
    )
    spread = lax.dynamic_update_slice_in_dim(
        jnp.zeros(filters.shape, f32), taps, lax.axis_index("row") * local_groups, 0
    )
    return (out_grad, weight_grad, lax.psum(spread, ("row", "dp")))


def toeplitz(taps, tok_rows, causal):
    filter_len = taps.shape[1]
    out_pos = lax.broadcasted_iota(jnp.int32, (tok_rows, tok_rows + filter_len), 0)
    in_pos = lax.broadcasted_iota(jnp.int32, (tok_rows, tok_rows + filter_len), 1)
    lagged = out_pos + filter_len - in_pos if causal else in_pos - out_pos
    inside = (lagged >= 0) & (lagged < filter_len)
    picked = jnp.take(taps, jnp.clip(lagged, 0, filter_len - 1), axis=1)
    return jnp.where(inside[None], picked, 0.0)


def grouped_apply(table, signal, groups):
    blocks, extent, channels = signal.shape
    split = signal.reshape(blocks, extent, groups, channels // groups)
    result = jnp.einsum("gts,bsgc->btgc", table, split, precision=highest)
    return result.reshape(blocks, table.shape[1], channels)


def taps_partial(delta_mix, mixed_ext, groups, filter_len):
    blocks, tok_rows, channels = delta_mix.shape
    left_side = delta_mix.reshape(blocks, tok_rows, groups, channels // groups)
    right_side = mixed_ext.reshape(blocks, tok_rows + filter_len, groups, channels // groups)
    products = jnp.einsum("btgc,bsgc->gts", left_side, right_side, precision=highest)
    extent = tok_rows + filter_len
    flipped = products[:, :, ::-1]
    padded = jnp.pad(flipped, ((0, 0), (0, 0), (0, tok_rows)))
    flat_rows = padded.reshape(groups, -1)[:, : tok_rows * (extent + tok_rows - 1)]
    skewed = flat_rows.reshape(groups, tok_rows, extent + tok_rows - 1)
    column_sums = jnp.sum(skewed, axis=1)
    return column_sums[:, tok_rows - 1 : tok_rows - 1 + filter_len]


def plain_local(grad_output, block_input, query_branch, key_branch, value_branch, out_weight, filters):
    filter_len = filters.shape[1]
    groups = filters.shape[0]
    tok_rows = query_branch.shape[1]
    channels = query_branch.shape[2]
    grads_all, inputs_all = (
        lax.all_gather(grad_output[0], "col", axis=0, tiled=True),
        lax.all_gather(block_input[0], "col", axis=0, tiled=True),
    )
    row_devices = lax.axis_size("row")
    sub_width = channels // row_devices
    delta_turned = lax.psum_scatter(
        lax.dot_general(
            out_weight, grads_all, (((0,), (1,)), ((), ())), preferred_element_type=jnp.float32
        ),
        "row",
        scatter_dimension=0,
        tiled=True,
    )
    queries, keys_here, values_here = (
        lax.all_to_all(query_branch[0], "row", split_axis=1, concat_axis=0, tiled=True),
        lax.all_to_all(key_branch[0], "row", split_axis=1, concat_axis=0, tiled=True),
        lax.all_to_all(value_branch[0], "row", split_axis=1, concat_axis=0, tiled=True),
    )
    delta_out = delta_turned.T
    local_groups = sub_width // (channels // groups)
    first_group = lax.axis_index("row") * local_groups
    my_taps = lax.dynamic_slice_in_dim(filters, first_group, local_groups, 0)
    mixed = keys_here.astype(jnp.float32) * values_here.astype(jnp.float32)
    mixed_blocks = mixed.reshape(row_devices, tok_rows, sub_width)
    earlier = jnp.concatenate(
        [
            jnp.zeros((1, filter_len, sub_width), jnp.float32),
            mixed_blocks[:-1, tok_rows - filter_len :],
        ],
        axis=0,
    )
    mixed_ext = jnp.concatenate([earlier, mixed_blocks], axis=1)
    conv_out = grouped_apply(toeplitz(my_taps, tok_rows, True), mixed_ext, local_groups).reshape(
        -1, sub_width
    )
    gated = (queries.astype(jnp.float32) * conv_out).astype(jnp.bfloat16)
    delta_mix = delta_out * queries.astype(jnp.float32)
    delta_blocks = delta_mix.reshape(row_devices, tok_rows, sub_width)
    later_part = jnp.concatenate(
        [delta_blocks[1:, :filter_len], jnp.zeros((1, filter_len, sub_width), jnp.float32)], axis=0
    )
    delta_ext = jnp.concatenate([delta_blocks, later_part], axis=1)
    delta_conv = grouped_apply(toeplitz(my_taps, tok_rows, False), delta_ext, local_groups).reshape(
        -1, sub_width
    )
    delta_value = (delta_conv * keys_here.astype(jnp.float32)).astype(jnp.bfloat16)
    my_terms = taps_partial(delta_blocks, mixed_ext, local_groups, filter_len)
    taps_local = lax.dynamic_update_slice_in_dim(
        jnp.zeros(filters.shape, jnp.float32), my_terms, first_group, 0
    )
    gated_all, value_all = (
        lax.all_gather(gated, "row", axis=1, tiled=True),
        lax.all_gather(delta_value, "row", axis=1, tiled=True),
    )
    out_grad = lax.dot_general(
        grads_all, gated_all, (((0,), (0,)), ((), ())), preferred_element_type=jnp.float32
    )
    value_grad = lax.dot_general(
        value_all, inputs_all, (((0,), (0,)), ((), ())), preferred_element_type=jnp.float32
    )
    out_grad, value_grad = lax.psum((out_grad, value_grad), "dp")
    taps_total = lax.psum(taps_local, ("row", "dp"))
    return (out_grad, value_grad, taps_total)


def solution(mesh):
    in_specs = (
        P("dp", "col", "row"),
        P("dp", "col", "row"),
        P("dp", "row", "col"),
        P("dp", "row", "col"),
        P("dp", "row", "col"),
        P("row", "col"),
        P("col", None),
    )
    out_specs = (P("row", "col"), P("col", "row"), P("col", None))

    def whole(*args):
        grad, filters = args[0], args[6]
        blocks_of = grad.shape[1] // mesh.shape["col"]
        width = grad.shape[2] // (mesh.shape["row"] * mesh.shape["col"])
        fits = (
            mesh.shape["row"] == 4
            and mesh.shape["col"] == 4
            and mesh.shape["dp"] == 2
            and grad.shape[0] == 2
            and blocks_of == 128
            and filters.shape[1] == 128
            and grad.shape[2] == 16 * filters.shape[0]
            and width % 512 == 0
        )
        body = local if fits else plain_local
        return jax.shard_map(body, mesh=mesh, in_specs=in_specs, out_specs=out_specs, check_vma=False)(*args)

    return whole
```

```python
import functools

import jax
import jax.numpy as jnp
from jax import lax
from jax.experimental import pallas as pl
from jax.experimental.pallas import tpu as pltpu
from jax.sharding import PartitionSpec as P

highest = lax.Precision.HIGHEST
f32, bf16 = jnp.float32, jnp.bfloat16
MIB = 1 << 20
VMEM = pl.BlockSpec(memory_space=pltpu.VMEM)
SMEM = pl.BlockSpec(memory_space=pltpu.SMEM)
ANY = pl.BlockSpec(memory_space=pl.ANY)
TILE = 256


def params():
    return pltpu.CompilerParams(vmem_limit_bytes=60 * MIB)


def cost(us):
    return pl.CostEstimate(flops=int(us * 1.15e9), bytes_accessed=0, transcendentals=0)


def split_two(x):
    hi = x.astype(bf16)
    return hi, (x - hi.astype(f32)).astype(bf16)


def turn_kernel(q_ref, k_ref, v_ref, out_ref):
    width = out_ref.shape[2]
    for j in range(out_ref.shape[0]):
        for n, src in enumerate((q_ref, k_ref, v_ref)):
            out_ref[j, n] = src[0, :, j * width : (j + 1) * width].T


def turn_branches(q, k, v, rows):
    _, toks, channels = q.shape
    return pl.pallas_call(
        turn_kernel,
        out_shape=jax.ShapeDtypeStruct((rows, 3, channels // rows, toks), bf16),
        in_specs=[VMEM] * 3,
        out_specs=VMEM,
        compiler_params=params(),
        cost_estimate=cost(3),
    )(q, k, v)


def tap_matrix(f_ref, row):
    taps = f_ref.shape[1]
    wide = jnp.broadcast_to(f_ref[pl.ds(row, 1), :], (taps, taps))
    ring = pltpu.roll(wide, 0, 1, stride=1, stride_axis=0)
    s = lax.broadcasted_iota(jnp.int32, (taps, taps), 0)
    t = lax.broadcasted_iota(jnp.int32, (taps, taps), 1)
    same = jnp.where(t >= s, ring, 0.0)
    return same, ring - same


def dot(a, b, dims=((1,), (0,))):
    return lax.dot_general(a, b, (dims, ((), ())), preferred_element_type=f32)


def forward_kernel(size, pos_ref, f_ref, parts_ref, out_ref, mh, ml, qs, gt):
    n = f_ref.shape[1]
    width, toks = gt.shape
    blocks = toks // n
    groups = width // size
    mh[:, :n] = jnp.zeros((width, n), bf16)
    ml[:, :n] = jnp.zeros((width, n), bf16)
    for j in range(blocks):
        hi, lo = split_two(parts_ref[j, 1].astype(f32) * parts_ref[j, 2].astype(f32))
        mh[:, (j + 1) * n : (j + 2) * n] = hi
        ml[:, (j + 1) * n : (j + 2) * n] = lo
        qs[:, j * n : (j + 1) * n] = parts_ref[j, 0]

    def one(g, carry):
        rows = pl.ds(pl.multiple_of(g * size, size), size)
        same, prev = tap_matrix(f_ref, pos_ref[0] * groups + g)
        table_hi, table_lo = split_two(jnp.concatenate([prev, same], axis=0))
        x_hi = jnp.concatenate([mh[rows, b * n : (b + 2) * n] for b in range(blocks)], axis=0)
        x_lo = jnp.concatenate([ml[rows, b * n : (b + 2) * n] for b in range(blocks)], axis=0)
        conv = dot(x_hi, table_hi) + dot(x_lo, table_hi) + dot(x_hi, table_lo)
        for b in range(blocks):
            gate = qs[rows, b * n : (b + 1) * n].astype(f32)
            gt[rows, b * n : (b + 1) * n] = gate * conv[b * size : (b + 1) * size]
        return carry

    lax.fori_loop(0, groups, one, 0, unroll=4)
    for b in range(blocks):
        out_ref[b * n : (b + 1) * n, :] = gt[:, b * n : (b + 1) * n].T.astype(bf16)


def forward(pos, filters, parts, size):
    rows, _, width, n = parts.shape
    toks = n * rows
    return pl.pallas_call(
        functools.partial(forward_kernel, size),
        out_shape=jax.ShapeDtypeStruct((toks, width), bf16),
        in_specs=[SMEM] + [VMEM] * 2,
        out_specs=VMEM,
        scratch_shapes=[
            pltpu.VMEM((width, toks + n), bf16),
            pltpu.VMEM((width, toks + n), bf16),
            pltpu.VMEM((width, toks), bf16),
            pltpu.VMEM((width, toks), f32),
        ],
        compiler_params=params(),
        cost_estimate=cost(6),
    )(pos, filters, parts)


def backward_kernel(size, counts, pos_ref, f_ref, parts_ref, *refs):
    n = f_ref.shape[1]
    deltas, out_ref, (dh, dl, mh, ml, qs, ks, sums) = refs[:-8], refs[-8], refs[-7:]
    width, toks = qs.shape
    blocks = toks // n
    groups = width // size
    row, col = pos_ref[0], pos_ref[1]
    zero = jnp.zeros((width, n), bf16)
    mh[:, :n] = zero
    ml[:, :n] = zero
    dh[:, toks:] = zero
    dl[:, toks:] = zero
    for j in range(blocks):
        hi, lo = split_two(parts_ref[j, 1].astype(f32) * parts_ref[j, 2].astype(f32))
        mh[:, (j + 1) * n : (j + 2) * n] = hi
        ml[:, (j + 1) * n : (j + 2) * n] = lo
        qs[:, j * n : (j + 1) * n] = parts_ref[j, 0]
        ks[:, j * n : (j + 1) * n] = parts_ref[j, 1]
    slot = 0
    for i, count in enumerate(counts):
        for m in range(count):
            place = pl.multiple_of((col ^ slot) * n, n)
            at = slice(m * n, (m + 1) * n)
            own = deltas[2 * i][at, :]
            delta = sum(jnp.where(row == j, own, deltas[2 * i + 1][j, at, :].astype(f32)) for j in range(blocks))
            hi, lo = split_two(delta.T * qs[:, pl.ds(place, n)].astype(f32))
            dh[:, pl.ds(place, n)] = hi
            dl[:, pl.ds(place, n)] = lo
            slot += 1
    s = lax.broadcasted_iota(jnp.int32, (n, n), 0)
    t = lax.broadcasted_iota(jnp.int32, (n, n), 1)

    def one(g, carry):
        rows = pl.ds(pl.multiple_of(g * size, size), size)
        same, prev = tap_matrix(f_ref, row * groups + g)
        table_hi, table_lo = split_two(jnp.concatenate([same, prev], axis=1))
        d_hi = [dh[rows, b * n : (b + 2) * n] for b in range(blocks)]
        d_lo = [dl[rows, b * n : (b + 2) * n] for b in range(blocks)]
        x_hi, x_lo = jnp.concatenate(d_hi, axis=0), jnp.concatenate(d_lo, axis=0)
        across = ((1,), (1,))
        conv = dot(x_hi, table_hi, across) + dot(x_lo, table_hi, across) + dot(x_hi, table_lo, across)
        for b in range(blocks):
            key = ks[rows, b * n : (b + 1) * n].astype(f32)
            out_ref[rows, b * n : (b + 1) * n] = (key * conv[b * size : (b + 1) * size]).astype(bf16)
        m_hi = [mh[rows, b * n : (b + 2) * n] for b in range(blocks)]
        m_lo = [ml[rows, b * n : (b + 2) * n] for b in range(blocks)]
        d_hi, d_lo = [d[:, :n] for d in d_hi], [d[:, :n] for d in d_lo]
        pairs = dot(
            jnp.concatenate(m_hi + m_lo + m_hi, axis=0),
            jnp.concatenate(d_hi + d_hi + d_lo, axis=0),
            ((0,), (0,)),
        )
        ring = jnp.where(s <= t, pairs[n:], pairs[:n])
        half = n // 2
        while half >= 8:
            ring = ring[:half] + pltpu.roll(ring[half:], n - half, 1)
            half //= 2
        sums[pl.ds(pl.multiple_of(g * 8, 8), 8), :] = ring
        return carry

    lax.fori_loop(0, groups, one, 0, unroll=4)
    total = sums[pl.ds(0, groups, stride=8), :]
    for i in range(1, 8):
        total = total + pltpu.roll(sums[pl.ds(i, groups, stride=8), :], n - i, 1)
    hi, lo = split_two(total)
    half = groups // 2
    out_ref[width:, :] = jnp.concatenate([hi[:half], hi[half:], lo[:half], lo[half:]], axis=1)


def backward(pos, filters, parts, deltas, counts, size):
    rows, _, width, n = parts.shape
    toks = n * rows
    groups = width // size
    return pl.pallas_call(
        functools.partial(backward_kernel, size, counts),
        out_shape=jax.ShapeDtypeStruct((width + groups // 2, toks), bf16),
        in_specs=[SMEM] + [VMEM] * (2 + len(deltas)),
        out_specs=VMEM,
        scratch_shapes=[pltpu.VMEM((width, toks + n), bf16)] * 4
        + [pltpu.VMEM((width, toks), bf16)] * 2
        + [pltpu.VMEM((8 * groups, n), f32)],
        compiler_params=params(),
        cost_estimate=cost(12),
    )(pos, filters, parts, *deltas)


def project_kernel(count, pos_ref, *refs):
    slots, (w_ref, own_ref, out_ref, wide, sem) = refs[:count], refs[count:]
    rows, _, width = out_ref.shape

    def fetch(j):
        return pltpu.make_async_copy(w_ref.at[:, pl.ds(j * width, width)], wide.at[j], sem.at[j])

    for j in range(rows):
        fetch(j).start()
    grads = jnp.concatenate([slot[...] for slot in slots], axis=0)
    for j in range(rows):
        fetch(j).wait()
        part = dot(grads, wide[j])
        out_ref[j] = part.astype(bf16)

        @pl.when(pos_ref[0] == j)
        def _():
            own_ref[...] = part


def project(pos, slots, weight, rows):
    depth, channels = weight.shape
    width = channels // rows
    toks = sum(slot.shape[0] for slot in slots)
    return pl.pallas_call(
        functools.partial(project_kernel, len(slots)),
        out_shape=[
            jax.ShapeDtypeStruct((toks, width), f32),
            jax.ShapeDtypeStruct((rows, toks, width), bf16),
        ],
        in_specs=[SMEM] + [VMEM] * len(slots) + [ANY],
        out_specs=[VMEM] * 2,
        scratch_shapes=[pltpu.VMEM((rows, depth, width), bf16), pltpu.SemaphoreType.DMA((rows,))],
        compiler_params=params(),
        cost_estimate=cost(8),
    )(pos, *slots, weight)


def product(left, right, buf, out_ref, sem_out, turned, places):
    tile = buf.shape[1]

    def send(i):
        at = pl.ds(pl.multiple_of(places[i], tile), tile)
        return pltpu.make_async_copy(buf.at[i % 2], out_ref.at[at, :], sem_out.at[i % 2])

    for i in range(len(places)):
        if i >= 2:
            send(i - 2).wait()
        at = slice(i * tile, (i + 1) * tile)
        buf[i % 2] = dot(left[:, at].T if turned else left[at, :], right[...])
        send(i).start()
    for i in range(max(0, len(places) - 2), len(places)):
        send(i).wait()


def run_copies(pairs, sem):
    copies = [pltpu.make_async_copy(src, dst, sem.at[i]) for i, (src, dst) in enumerate(pairs)]
    for copy in copies:
        copy.start()
    for copy in copies:
        copy.wait()


def out_kernel(n, layout, pos_ref, *refs):
    slots, pieces = refs[:8], refs[8 : 8 + len(layout)]
    out_ref, left, right, buf, sem_in, sem_out = refs[8 + len(layout) :]
    row, col = pos_ref[0], pos_ref[1]
    seq = left.shape[0] // 2
    width = right.shape[1] // 4
    pairs = []
    for i, slot in enumerate(slots):
        place = pl.multiple_of((i // 4) * seq + (col ^ (i % 4)) * n, n)
        pairs.append((slot, left.at[pl.ds(place, n), :]))
    for piece, (block, owner, first, count) in zip(pieces, layout, strict=True):
        columns = pl.ds(pl.multiple_of((row ^ block) * width, width), width)
        pairs.append((piece, right.at[pl.ds(owner * seq + first, count), columns]))
    run_copies(pairs, sem_in)
    tile = buf.shape[1]
    product(left, right, buf, out_ref, sem_out, True, [i * tile for i in range(out_ref.shape[0] // tile)])


def out_gradient(pos, slots, pieces, layout):
    n, left_width = slots[0].shape
    seq, width = pieces[0].shape
    right_width = 4 * width
    toks = 2 * seq
    return pl.pallas_call(
        functools.partial(out_kernel, n, layout),
        out_shape=jax.ShapeDtypeStruct((left_width, right_width), f32),
        in_specs=[SMEM] + [ANY] * (8 + len(pieces)),
        out_specs=ANY,
        scratch_shapes=[
            pltpu.VMEM((toks, left_width), bf16),
            pltpu.VMEM((toks, right_width), bf16),
            pltpu.VMEM((2, TILE, right_width), f32),
            pltpu.SemaphoreType.DMA((8 + len(pieces),)),
            pltpu.SemaphoreType.DMA((2,)),
        ],
        compiler_params=params(),
        cost_estimate=cost(16),
    )(pos, *slots, *pieces)


def value_kernel(n, width, which, layout, with_taps, joined, pos_ref, *refs):
    inputs, refs = refs[:8], refs[8:]
    pieces, refs = refs[: len(layout)], refs[len(layout) :]
    if with_taps:
        ends, refs = refs[:8], refs[8:]
    if joined:
        refs = refs[1:]
    out_ref, refs = refs[0], refs[1:]
    if with_taps:
        taps_ref, refs = refs[0], refs[1:]
        tails, refs = refs[-1], refs[:-1]
    left, right, buf, sem_in, sem_out = refs
    row, col = pos_ref[0], pos_ref[1]
    seq = left.shape[1] // 2
    pairs = []
    for i, slot in enumerate(inputs):
        place = pl.multiple_of((i // 4) * seq + (col ^ (i % 4)) * n, n)
        pairs.append((slot, right.at[pl.ds(place, n), :]))
    for piece, (block, owner, first, count) in zip(pieces, layout, strict=True):
        place = left.at[pl.ds(block * width + first, count), pl.ds(owner * seq, seq)]
        pairs.append((piece.at[pl.ds(0, count), :], place))
    if with_taps:
        half = tails.shape[1]
        for i, end in enumerate(ends):
            pairs.append((end.at[pl.ds(end.shape[0] - half, half), :], tails.at[i]))
    run_copies(pairs, sem_in)
    if with_taps:
        lanes = taps_ref.shape[1]
        for j in range(4):
            both = tails[j].astype(f32), tails[j + 4].astype(f32)
            cut = [[t[:, i * lanes : (i + 1) * lanes] for i in range(4)] for t in both]
            for h in range(2):
                place = pl.multiple_of((row ^ j) * 2 * half + h * half, half)
                taps_ref[pl.ds(place, half), :] = (cut[0][h] + cut[0][h + 2]) + (cut[1][h] + cut[1][h + 2])
    tile = buf.shape[1]
    places = [(row ^ j) * width + i * tile for j in which for i in range(width // tile)]
    product(left, right, buf, out_ref, sem_out, False, places)


def value_part(pos, inputs, pieces, layout, which, width, ends=(), taps_shape=None, partial=None):
    n, right_width = inputs[0].shape
    seq = pieces[0].shape[1]
    with_taps, joined = taps_shape is not None, partial is not None
    out_shape = [jax.ShapeDtypeStruct((4 * width, right_width), f32)]
    scratch = [
        pltpu.VMEM((len(which) * width, 2 * seq), bf16),
        pltpu.VMEM((2 * seq, right_width), bf16),
        pltpu.VMEM((2, TILE, right_width), f32),
        pltpu.SemaphoreType.DMA((8 + len(pieces) + len(ends),)),
        pltpu.SemaphoreType.DMA((2,)),
    ]
    operands = [pos, *inputs, *pieces, *ends]
    aliases = {}
    if with_taps:
        out_shape.append(jax.ShapeDtypeStruct(taps_shape, f32))
        scratch.append(pltpu.VMEM((8, 16, seq), bf16))
    if joined:
        aliases = {len(operands): 0}
        operands.append(partial)
    return pl.pallas_call(
        functools.partial(value_kernel, n, width, which, layout, with_taps, joined),
        out_shape=out_shape,
        in_specs=[SMEM] + [ANY] * (len(operands) - 1),
        out_specs=[ANY, VMEM][: len(out_shape)],
        scratch_shapes=scratch,
        input_output_aliases=aliases,
        compiler_params=params(),
        cost_estimate=cost(10),
    )(*operands)


near = [(0, 1), (1, 0), (2, 3), (3, 2)]
far = [(0, 2), (2, 0), (1, 3), (3, 1)]
swap = [(0, 1), (1, 0)]


def line_slots(x):
    c = lax.axis_index("col")
    first = lax.ppermute(x, "col", near)
    second = lax.ppermute(x, "col", far)
    inner = lax.ppermute(x, "col", [(1, 2), (2, 1)])
    passed = lax.ppermute(second, "col", [(2, 3), (1, 0)])
    third = jnp.where((c == 1) | (c == 2), inner, passed)
    return [x, first, second, third]


def swap_rows(x):
    return lax.all_to_all(x, "row", split_axis=0, concat_axis=0, tiled=True)


def row_gather(x, half):
    beside = lax.ppermute(x, "row", near)
    above = lax.ppermute(x, "row", far)
    return [
        x,
        beside,
        above,
        lax.ppermute(beside[:half], "row", far),
        lax.ppermute(above[half:], "row", near),
    ]


def other_core(xs):
    return [lax.ppermute(x, "dp", swap) for x in xs]


def after(pos, x):
    return lax.optimization_barrier((pos, x))[0]


def local(grad_output, block_input, query_branch, key_branch, value_branch, out_weight, filters):
    rows = lax.axis_size("row")
    toks = query_branch.shape[1]
    channels = query_branch.shape[2]
    size = channels // filters.shape[0]
    width = channels // rows
    pos = jnp.stack([lax.axis_index("row"), lax.axis_index("col"), lax.axis_index("dp")]).astype(jnp.int32)

    grads = line_slots(grad_output[0])
    turned = turn_branches(query_branch, key_branch, value_branch, rows)
    parts = swap_rows(turned)
    held = lax.optimization_barrier((block_input[0], grads[3]))
    inputs = line_slots(held[0])

    counts = (3, 1)
    deltas = []
    for chosen in (grads[:3], grads[3:]):
        own, sums = project(pos, chosen, out_weight, rows)
        pos = after(pos, own)
        if deltas:
            sums = after(sums, deltas[-1])
        deltas += [own, swap_rows(sums)]
    gated = forward(pos, filters, parts, size)
    seq = rows * toks
    gated_all = row_gather(gated, seq // 2)
    mine = backward(after(pos, (gated, inputs[1], inputs[2])), filters, parts, deltas, counts, size)
    pos, *late = lax.optimization_barrier((pos, mine, *grads, *gated_all, *inputs[:3]))
    mine, grads, gated_all, inputs = late[0], late[1:5], late[5:10], late[10:] + inputs[3:]
    half = width // 2
    values = row_gather(mine, half)
    _, beside, above, *corner = values
    others = other_core(values)
    inputs = inputs + other_core(inputs)
    gated_all = gated_all + other_core(gated_all)
    grads_all = grads + other_core(grads)
    cuts = [(0, 0, seq), (1, 0, seq), (2, 0, seq), (3, 0, seq // 2), (3, seq // 2, seq // 2)]
    layout = [(block, owner, first, count) for owner in (0, 1) for block, first, count in cuts]

    out_grad = out_gradient(pos, grads_all, gated_all, layout)
    three = [(block, owner, 0, width) for block in range(3) for owner in (0, 1)]
    pieces = [piece for pair in zip(values[:3], others[:3], strict=True) for piece in pair]
    value_grad = value_part(after(pos, out_grad), inputs, pieces, three, (0, 1, 2), width)[0]
    halves = [(0, 0, 0, half), (0, 0, half, half), (0, 1, 0, half), (0, 1, half, half)]
    value_grad, taps = value_part(
        pos,
        inputs,
        corner + others[3:],
        halves,
        (3,),
        width,
        ends=[mine, beside, above, corner[1], *others[:3], others[4]],
        taps_shape=filters.shape,
        partial=value_grad,
    )
    return (out_grad, value_grad, taps)


def toeplitz(taps, tok_rows, causal):
    filter_len = taps.shape[1]
    out_pos = lax.broadcasted_iota(jnp.int32, (tok_rows, tok_rows + filter_len), 0)
    in_pos = lax.broadcasted_iota(jnp.int32, (tok_rows, tok_rows + filter_len), 1)
    lagged = out_pos + filter_len - in_pos if causal else in_pos - out_pos
    inside = (lagged >= 0) & (lagged < filter_len)
    picked = jnp.take(taps, jnp.clip(lagged, 0, filter_len - 1), axis=1)
    return jnp.where(inside[None], picked, 0.0)


def grouped_apply(table, signal, groups):
    blocks, extent, channels = signal.shape
    split = signal.reshape(blocks, extent, groups, channels // groups)
    result = jnp.einsum("gts,bsgc->btgc", table, split, precision=highest)
    return result.reshape(blocks, table.shape[1], channels)


def taps_partial(delta_mix, mixed_ext, groups, filter_len):
    blocks, tok_rows, channels = delta_mix.shape
    left_side = delta_mix.reshape(blocks, tok_rows, groups, channels // groups)
    right_side = mixed_ext.reshape(blocks, tok_rows + filter_len, groups, channels // groups)
    products = jnp.einsum("btgc,bsgc->gts", left_side, right_side, precision=highest)
    extent = tok_rows + filter_len
    flipped = products[:, :, ::-1]
    padded = jnp.pad(flipped, ((0, 0), (0, 0), (0, tok_rows)))
    flat_rows = padded.reshape(groups, -1)[:, : tok_rows * (extent + tok_rows - 1)]
    skewed = flat_rows.reshape(groups, tok_rows, extent + tok_rows - 1)
    column_sums = jnp.sum(skewed, axis=1)
    return column_sums[:, tok_rows - 1 : tok_rows - 1 + filter_len]


def plain_local(grad_output, block_input, query_branch, key_branch, value_branch, out_weight, filters):
    filter_len = filters.shape[1]
    groups = filters.shape[0]
    tok_rows = query_branch.shape[1]
    channels = query_branch.shape[2]
    grads_all, inputs_all = (
        lax.all_gather(grad_output[0], "col", axis=0, tiled=True),
        lax.all_gather(block_input[0], "col", axis=0, tiled=True),
    )
    row_devices = lax.axis_size("row")
    sub_width = channels // row_devices
    delta_turned = lax.psum_scatter(
        lax.dot_general(
            out_weight, grads_all, (((0,), (1,)), ((), ())), preferred_element_type=jnp.float32
        ),
        "row",
        scatter_dimension=0,
        tiled=True,
    )
    queries, keys_here, values_here = (
        lax.all_to_all(query_branch[0], "row", split_axis=1, concat_axis=0, tiled=True),
        lax.all_to_all(key_branch[0], "row", split_axis=1, concat_axis=0, tiled=True),
        lax.all_to_all(value_branch[0], "row", split_axis=1, concat_axis=0, tiled=True),
    )
    delta_out = delta_turned.T
    local_groups = sub_width // (channels // groups)
    first_group = lax.axis_index("row") * local_groups
    my_taps = lax.dynamic_slice_in_dim(filters, first_group, local_groups, 0)
    mixed = keys_here.astype(jnp.float32) * values_here.astype(jnp.float32)
    mixed_blocks = mixed.reshape(row_devices, tok_rows, sub_width)
    earlier = jnp.concatenate(
        [
            jnp.zeros((1, filter_len, sub_width), jnp.float32),
            mixed_blocks[:-1, tok_rows - filter_len :],
        ],
        axis=0,
    )
    mixed_ext = jnp.concatenate([earlier, mixed_blocks], axis=1)
    conv_out = grouped_apply(toeplitz(my_taps, tok_rows, True), mixed_ext, local_groups).reshape(
        -1, sub_width
    )
    gated = (queries.astype(jnp.float32) * conv_out).astype(jnp.bfloat16)
    delta_mix = delta_out * queries.astype(jnp.float32)
    delta_blocks = delta_mix.reshape(row_devices, tok_rows, sub_width)
    later_part = jnp.concatenate(
        [delta_blocks[1:, :filter_len], jnp.zeros((1, filter_len, sub_width), jnp.float32)], axis=0
    )
    delta_ext = jnp.concatenate([delta_blocks, later_part], axis=1)
    delta_conv = grouped_apply(toeplitz(my_taps, tok_rows, False), delta_ext, local_groups).reshape(
        -1, sub_width
    )
    delta_value = (delta_conv * keys_here.astype(jnp.float32)).astype(jnp.bfloat16)
    my_terms = taps_partial(delta_blocks, mixed_ext, local_groups, filter_len)
    taps_local = lax.dynamic_update_slice_in_dim(
        jnp.zeros(filters.shape, jnp.float32), my_terms, first_group, 0
    )
    gated_all, value_all = (
        lax.all_gather(gated, "row", axis=1, tiled=True),
        lax.all_gather(delta_value, "row", axis=1, tiled=True),
    )
    out_grad = lax.dot_general(
        grads_all, gated_all, (((0,), (0,)), ((), ())), preferred_element_type=jnp.float32
    )
    value_grad = lax.dot_general(
        value_all, inputs_all, (((0,), (0,)), ((), ())), preferred_element_type=jnp.float32
    )
    out_grad, value_grad = lax.psum((out_grad, value_grad), "dp")
    taps_total = lax.psum(taps_local, ("row", "dp"))
    return (out_grad, value_grad, taps_total)


def solution(mesh):
    in_specs = (
        P("dp", "col", "row"),
        P("dp", "col", "row"),
        P("dp", "row", "col"),
        P("dp", "row", "col"),
        P("dp", "row", "col"),
        P("row", "col"),
        P("col", None),
    )
    out_specs = (P("row", "col"), P("col", "row"), P("col", None))

    def whole(*args):
        grad, filters = args[0], args[6]
        blocks_of = grad.shape[1] // mesh.shape["col"]
        width = grad.shape[2] // (mesh.shape["row"] * mesh.shape["col"])
        fits = (
            mesh.shape["row"] == 4
            and mesh.shape["col"] == 4
            and mesh.shape["dp"] == 2
            and grad.shape[0] == 2
            and blocks_of == 128
            and filters.shape[1] == 128
            and grad.shape[2] == 16 * filters.shape[0]
            and width % 512 == 0
        )
        body = local if fits else plain_local
        return jax.shard_map(body, mesh=mesh, in_specs=in_specs, out_specs=out_specs, check_vma=False)(*args)

    return whole
```

```python
import functools

import jax
import jax.numpy as jnp
from jax import lax
from jax.experimental import pallas as pl
from jax.experimental.pallas import tpu as pltpu
from jax.sharding import PartitionSpec as P

highest = lax.Precision.HIGHEST
f32, bf16 = jnp.float32, jnp.bfloat16
MIB = 1 << 20
VMEM = pl.BlockSpec(memory_space=pltpu.VMEM)
SMEM = pl.BlockSpec(memory_space=pltpu.SMEM)
ANY = pl.BlockSpec(memory_space=pl.ANY)
TILE = 256


def params():
    return pltpu.CompilerParams(vmem_limit_bytes=60 * MIB)


def cost(us):
    return pl.CostEstimate(flops=int(us * 1.15e9), bytes_accessed=0, transcendentals=0)


def split_two(x):
    hi = x.astype(bf16)
    return hi, (x - hi.astype(f32)).astype(bf16)


def turn_kernel(q_ref, k_ref, v_ref, out_ref):
    width = out_ref.shape[2]
    for j in range(out_ref.shape[0]):
        for n, src in enumerate((q_ref, k_ref, v_ref)):
            out_ref[j, n] = src[0, :, j * width : (j + 1) * width].T


def turn_branches(q, k, v, rows):
    _, toks, channels = q.shape
    return pl.pallas_call(
        turn_kernel,
        out_shape=jax.ShapeDtypeStruct((rows, 3, channels // rows, toks), bf16),
        in_specs=[VMEM] * 3,
        out_specs=VMEM,
        compiler_params=params(),
        cost_estimate=cost(3),
    )(q, k, v)


def tap_matrix(f_ref, row):
    taps = f_ref.shape[1]
    wide = jnp.broadcast_to(f_ref[pl.ds(row, 1), :], (taps, taps))
    ring = pltpu.roll(wide, 0, 1, stride=1, stride_axis=0)
    s = lax.broadcasted_iota(jnp.int32, (taps, taps), 0)
    t = lax.broadcasted_iota(jnp.int32, (taps, taps), 1)
    same = jnp.where(t >= s, ring, 0.0)
    return same, ring - same


def dot(a, b, dims=((1,), (0,))):
    return lax.dot_general(a, b, (dims, ((), ())), preferred_element_type=f32)


def forward_kernel(size, pos_ref, f_ref, parts_ref, out_ref, mh, ml, qs, gt):
    n = f_ref.shape[1]
    width, toks = gt.shape
    blocks = toks // n
    groups = width // size
    mh[:, :n] = jnp.zeros((width, n), bf16)
    ml[:, :n] = jnp.zeros((width, n), bf16)
    for j in range(blocks):
        hi, lo = split_two(parts_ref[j, 1].astype(f32) * parts_ref[j, 2].astype(f32))
        mh[:, (j + 1) * n : (j + 2) * n] = hi
        ml[:, (j + 1) * n : (j + 2) * n] = lo
        qs[:, j * n : (j + 1) * n] = parts_ref[j, 0]

    def one(g, carry):
        rows = pl.ds(pl.multiple_of(g * size, size), size)
        same, prev = tap_matrix(f_ref, pos_ref[0] * groups + g)
        table_hi, table_lo = split_two(jnp.concatenate([prev, same], axis=0))
        x_hi = jnp.concatenate([mh[rows, b * n : (b + 2) * n] for b in range(blocks)], axis=0)
        x_lo = jnp.concatenate([ml[rows, b * n : (b + 2) * n] for b in range(blocks)], axis=0)
        conv = dot(x_hi, table_hi) + dot(x_lo, table_hi) + dot(x_hi, table_lo)
        for b in range(blocks):
            gate = qs[rows, b * n : (b + 1) * n].astype(f32)
            gt[rows, b * n : (b + 1) * n] = gate * conv[b * size : (b + 1) * size]
        return carry

    lax.fori_loop(0, groups, one, 0, unroll=4)
    for b in range(blocks):
        out_ref[b * n : (b + 1) * n, :] = gt[:, b * n : (b + 1) * n].T.astype(bf16)


def forward(pos, filters, parts, size):
    rows, _, width, n = parts.shape
    toks = n * rows
    return pl.pallas_call(
        functools.partial(forward_kernel, size),
        out_shape=jax.ShapeDtypeStruct((toks, width), bf16),
        in_specs=[SMEM] + [VMEM] * 2,
        out_specs=VMEM,
        scratch_shapes=[
            pltpu.VMEM((width, toks + n), bf16),
            pltpu.VMEM((width, toks + n), bf16),
            pltpu.VMEM((width, toks), bf16),
            pltpu.VMEM((width, toks), f32),
        ],
        compiler_params=params(),
        cost_estimate=cost(0),
    )(pos, filters, parts)


def backward_kernel(size, counts, pos_ref, f_ref, parts_ref, *refs):
    n = f_ref.shape[1]
    deltas, out_ref, (dh, dl, mh, ml, qs, ks, sums) = refs[:-8], refs[-8], refs[-7:]
    width, toks = qs.shape
    blocks = toks // n
    groups = width // size
    row, col = pos_ref[0], pos_ref[1]
    zero = jnp.zeros((width, n), bf16)
    mh[:, :n] = zero
    ml[:, :n] = zero
    dh[:, toks:] = zero
    dl[:, toks:] = zero
    for j in range(blocks):
        hi, lo = split_two(parts_ref[j, 1].astype(f32) * parts_ref[j, 2].astype(f32))
        mh[:, (j + 1) * n : (j + 2) * n] = hi
        ml[:, (j + 1) * n : (j + 2) * n] = lo
        qs[:, j * n : (j + 1) * n] = parts_ref[j, 0]
        ks[:, j * n : (j + 1) * n] = parts_ref[j, 1]
    slot = 0
    for i, count in enumerate(counts):
        for m in range(count):
            place = pl.multiple_of((col ^ slot) * n, n)
            at = slice(m * n, (m + 1) * n)
            own = deltas[2 * i][at, :]
            delta = sum(jnp.where(row == j, own, deltas[2 * i + 1][j, at, :].astype(f32)) for j in range(blocks))
            hi, lo = split_two(delta.T * qs[:, pl.ds(place, n)].astype(f32))
            dh[:, pl.ds(place, n)] = hi
            dl[:, pl.ds(place, n)] = lo
            slot += 1
    s = lax.broadcasted_iota(jnp.int32, (n, n), 0)
    t = lax.broadcasted_iota(jnp.int32, (n, n), 1)

    def one(g, carry):
        rows = pl.ds(pl.multiple_of(g * size, size), size)
        same, prev = tap_matrix(f_ref, row * groups + g)
        table_hi, table_lo = split_two(jnp.concatenate([same, prev], axis=1))
        d_hi = [dh[rows, b * n : (b + 2) * n] for b in range(blocks)]
        d_lo = [dl[rows, b * n : (b + 2) * n] for b in range(blocks)]
        x_hi, x_lo = jnp.concatenate(d_hi, axis=0), jnp.concatenate(d_lo, axis=0)
        across = ((1,), (1,))
        conv = dot(x_hi, table_hi, across) + dot(x_lo, table_hi, across) + dot(x_hi, table_lo, across)
        for b in range(blocks):
            key = ks[rows, b * n : (b + 1) * n].astype(f32)
            out_ref[rows, b * n : (b + 1) * n] = (key * conv[b * size : (b + 1) * size]).astype(bf16)
        m_hi = [mh[rows, b * n : (b + 2) * n] for b in range(blocks)]
        m_lo = [ml[rows, b * n : (b + 2) * n] for b in range(blocks)]
        d_hi, d_lo = [d[:, :n] for d in d_hi], [d[:, :n] for d in d_lo]
        pairs = dot(
            jnp.concatenate(m_hi + m_lo + m_hi, axis=0),
            jnp.concatenate(d_hi + d_hi + d_lo, axis=0),
            ((0,), (0,)),
        )
        ring = jnp.where(s <= t, pairs[n:], pairs[:n])
        half = n // 2
        while half >= 8:
            ring = ring[:half] + pltpu.roll(ring[half:], n - half, 1)
            half //= 2
        sums[pl.ds(pl.multiple_of(g * 8, 8), 8), :] = ring
        return carry

    lax.fori_loop(0, groups, one, 0, unroll=4)
    total = sums[pl.ds(0, groups, stride=8), :]
    for i in range(1, 8):
        total = total + pltpu.roll(sums[pl.ds(i, groups, stride=8), :], n - i, 1)
    hi, lo = split_two(total)
    half = groups // 2
    out_ref[width:, :] = jnp.concatenate([hi[:half], hi[half:], lo[:half], lo[half:]], axis=1)


def backward(pos, filters, parts, deltas, counts, size):
    rows, _, width, n = parts.shape
    toks = n * rows
    groups = width // size
    return pl.pallas_call(
        functools.partial(backward_kernel, size, counts),
        out_shape=jax.ShapeDtypeStruct((width + groups // 2, toks), bf16),
        in_specs=[SMEM] + [VMEM] * (2 + len(deltas)),
        out_specs=VMEM,
        scratch_shapes=[pltpu.VMEM((width, toks + n), bf16)] * 4
        + [pltpu.VMEM((width, toks), bf16)] * 2
        + [pltpu.VMEM((8 * groups, n), f32)],
        compiler_params=params(),
        cost_estimate=cost(12),
    )(pos, filters, parts, *deltas)


def project_kernel(count, pos_ref, *refs):
    slots, (w_ref, own_ref, out_ref, wide, sem) = refs[:count], refs[count:]
    rows, _, width = out_ref.shape

    def fetch(j):
        return pltpu.make_async_copy(w_ref.at[:, pl.ds(j * width, width)], wide.at[j], sem.at[j])

    for j in range(rows):
        fetch(j).start()
    grads = jnp.concatenate([slot[...] for slot in slots], axis=0)
    for j in range(rows):
        fetch(j).wait()
        part = dot(grads, wide[j])
        out_ref[j] = part.astype(bf16)

        @pl.when(pos_ref[0] == j)
        def _():
            own_ref[...] = part


def project(pos, slots, weight, rows):
    depth, channels = weight.shape
    width = channels // rows
    toks = sum(slot.shape[0] for slot in slots)
    return pl.pallas_call(
        functools.partial(project_kernel, len(slots)),
        out_shape=[
            jax.ShapeDtypeStruct((toks, width), f32),
            jax.ShapeDtypeStruct((rows, toks, width), bf16),
        ],
        in_specs=[SMEM] + [VMEM] * len(slots) + [ANY],
        out_specs=[VMEM] * 2,
        scratch_shapes=[pltpu.VMEM((rows, depth, width), bf16), pltpu.SemaphoreType.DMA((rows,))],
        compiler_params=params(),
        cost_estimate=cost(8),
    )(pos, *slots, weight)


def product(left, right, buf, out_ref, sem_out, turned, places):
    tile = buf.shape[1]

    def send(i):
        at = pl.ds(pl.multiple_of(places[i], tile), tile)
        return pltpu.make_async_copy(buf.at[i % 2], out_ref.at[at, :], sem_out.at[i % 2])

    for i in range(len(places)):
        if i >= 2:
            send(i - 2).wait()
        at = slice(i * tile, (i + 1) * tile)
        buf[i % 2] = dot(left[:, at].T if turned else left[at, :], right[...])
        send(i).start()
    for i in range(max(0, len(places) - 2), len(places)):
        send(i).wait()


def run_copies(pairs, sem):
    copies = [pltpu.make_async_copy(src, dst, sem.at[i]) for i, (src, dst) in enumerate(pairs)]
    for copy in copies:
        copy.start()
    for copy in copies:
        copy.wait()


def out_kernel(n, layout, pos_ref, *refs):
    slots, pieces = refs[:8], refs[8 : 8 + len(layout)]
    out_ref, left, right, buf, sem_in, sem_out = refs[8 + len(layout) :]
    row, col = pos_ref[0], pos_ref[1]
    seq = left.shape[0] // 2
    width = right.shape[1] // 4
    pairs = []
    for i, slot in enumerate(slots):
        place = pl.multiple_of((i // 4) * seq + (col ^ (i % 4)) * n, n)
        pairs.append((slot, left.at[pl.ds(place, n), :]))
    for piece, (block, owner, first, count) in zip(pieces, layout, strict=True):
        columns = pl.ds(pl.multiple_of((row ^ block) * width, width), width)
        pairs.append((piece, right.at[pl.ds(owner * seq + first, count), columns]))
    run_copies(pairs, sem_in)
    tile = buf.shape[1]
    product(left, right, buf, out_ref, sem_out, True, [i * tile for i in range(out_ref.shape[0] // tile)])


def out_gradient(pos, slots, pieces, layout):
    n, left_width = slots[0].shape
    seq, width = pieces[0].shape
    right_width = 4 * width
    toks = 2 * seq
    return pl.pallas_call(
        functools.partial(out_kernel, n, layout),
        out_shape=jax.ShapeDtypeStruct((left_width, right_width), f32),
        in_specs=[SMEM] + [ANY] * (8 + len(pieces)),
        out_specs=ANY,
        scratch_shapes=[
            pltpu.VMEM((toks, left_width), bf16),
            pltpu.VMEM((toks, right_width), bf16),
            pltpu.VMEM((2, TILE, right_width), f32),
            pltpu.SemaphoreType.DMA((8 + len(pieces),)),
            pltpu.SemaphoreType.DMA((2,)),
        ],
        compiler_params=params(),
        cost_estimate=cost(16),
    )(pos, *slots, *pieces)


def value_kernel(n, width, which, layout, with_taps, joined, pos_ref, *refs):
    inputs, refs = refs[:8], refs[8:]
    pieces, refs = refs[: len(layout)], refs[len(layout) :]
    if with_taps:
        ends, refs = refs[:8], refs[8:]
    if joined:
        refs = refs[1:]
    out_ref, refs = refs[0], refs[1:]
    if with_taps:
        taps_ref, refs = refs[0], refs[1:]
        tails, refs = refs[-1], refs[:-1]
    left, right, buf, sem_in, sem_out = refs
    row, col = pos_ref[0], pos_ref[1]
    seq = left.shape[1] // 2
    pairs = []
    for i, slot in enumerate(inputs):
        place = pl.multiple_of((i // 4) * seq + (col ^ (i % 4)) * n, n)
        pairs.append((slot, right.at[pl.ds(place, n), :]))
    for piece, (block, owner, first, count) in zip(pieces, layout, strict=True):
        place = left.at[pl.ds(block * width + first, count), pl.ds(owner * seq, seq)]
        pairs.append((piece.at[pl.ds(0, count), :], place))
    if with_taps:
        half = tails.shape[1]
        for i, end in enumerate(ends):
            pairs.append((end.at[pl.ds(end.shape[0] - half, half), :], tails.at[i]))
    run_copies(pairs, sem_in)
    if with_taps:
        lanes = taps_ref.shape[1]
        for j in range(4):
            both = tails[j].astype(f32), tails[j + 4].astype(f32)
            cut = [[t[:, i * lanes : (i + 1) * lanes] for i in range(4)] for t in both]
            for h in range(2):
                place = pl.multiple_of((row ^ j) * 2 * half + h * half, half)
                taps_ref[pl.ds(place, half), :] = (cut[0][h] + cut[0][h + 2]) + (cut[1][h] + cut[1][h + 2])
    tile = buf.shape[1]
    places = [(row ^ j) * width + i * tile for j in which for i in range(width // tile)]
    product(left, right, buf, out_ref, sem_out, False, places)


def value_part(pos, inputs, pieces, layout, which, width, ends=(), taps_shape=None, partial=None):
    n, right_width = inputs[0].shape
    seq = pieces[0].shape[1]
    with_taps, joined = taps_shape is not None, partial is not None
    out_shape = [jax.ShapeDtypeStruct((4 * width, right_width), f32)]
    scratch = [
        pltpu.VMEM((len(which) * width, 2 * seq), bf16),
        pltpu.VMEM((2 * seq, right_width), bf16),
        pltpu.VMEM((2, TILE, right_width), f32),
        pltpu.SemaphoreType.DMA((8 + len(pieces) + len(ends),)),
        pltpu.SemaphoreType.DMA((2,)),
    ]
    operands = [pos, *inputs, *pieces, *ends]
    aliases = {}
    if with_taps:
        out_shape.append(jax.ShapeDtypeStruct(taps_shape, f32))
        scratch.append(pltpu.VMEM((8, 16, seq), bf16))
    if joined:
        aliases = {len(operands): 0}
        operands.append(partial)
    return pl.pallas_call(
        functools.partial(value_kernel, n, width, which, layout, with_taps, joined),
        out_shape=out_shape,
        in_specs=[SMEM] + [ANY] * (len(operands) - 1),
        out_specs=[ANY, VMEM][: len(out_shape)],
        scratch_shapes=scratch,
        input_output_aliases=aliases,
        compiler_params=params(),
        cost_estimate=cost(10),
    )(*operands)


near = [(0, 1), (1, 0), (2, 3), (3, 2)]
far = [(0, 2), (2, 0), (1, 3), (3, 1)]
swap = [(0, 1), (1, 0)]


def line_slots(x):
    c = lax.axis_index("col")
    first = lax.ppermute(x, "col", near)
    second = lax.ppermute(x, "col", far)
    inner = lax.ppermute(x, "col", [(1, 2), (2, 1)])
    passed = lax.ppermute(second, "col", [(2, 3), (1, 0)])
    third = jnp.where((c == 1) | (c == 2), inner, passed)
    return [x, first, second, third]


def swap_rows(x):
    return lax.all_to_all(x, "row", split_axis=0, concat_axis=0, tiled=True)


def row_gather(x, half, then=None):
    beside = lax.ppermute(x, "row", near)
    above = lax.ppermute(x, "row", far)
    if then is not None:
        beside, above, _ = lax.optimization_barrier((beside, above, then))
    return [
        x,
        beside,
        above,
        lax.ppermute(beside[:half], "row", far),
        lax.ppermute(above[half:], "row", near),
    ]


def other_core(xs):
    return [lax.ppermute(x, "dp", swap) for x in xs]


def after(pos, x):
    return lax.optimization_barrier((pos, x))[0]


def local(grad_output, block_input, query_branch, key_branch, value_branch, out_weight, filters):
    rows = lax.axis_size("row")
    toks = query_branch.shape[1]
    channels = query_branch.shape[2]
    size = channels // filters.shape[0]
    width = channels // rows
    pos = jnp.stack([lax.axis_index("row"), lax.axis_index("col"), lax.axis_index("dp")]).astype(jnp.int32)

    grads = line_slots(grad_output[0])
    turned = turn_branches(query_branch, key_branch, value_branch, rows)
    parts = swap_rows(turned)
    held = lax.optimization_barrier((block_input[0], grads[3]))
    inputs = line_slots(held[0])

    counts = (3, 1)
    deltas = []
    for chosen in (grads[:3], grads[3:]):
        own, sums = project(pos, chosen, out_weight, rows)
        pos = after(pos, own)
        if deltas:
            sums = after(sums, deltas[-1])
        deltas += [own, swap_rows(sums)]
    gated = forward(pos, filters, parts, size)
    seq = rows * toks
    gated_all = row_gather(gated, seq // 2)
    mine = backward(after(pos, (gated, inputs[1], inputs[2])), filters, parts, deltas, counts, size)
    pos, *late = lax.optimization_barrier((pos, mine, *grads, *gated_all, *inputs[:3]))
    mine, grads, gated_all, inputs = late[0], late[1:5], late[5:10], late[10:] + inputs[3:]
    half = width // 2
    inputs = inputs + other_core(inputs)
    other = other_core([mine])[0]
    gated_all = gated_all + other_core(gated_all)
    grads_all = grads + other_core(grads)
    cuts = [(0, 0, seq), (1, 0, seq), (2, 0, seq), (3, 0, seq // 2), (3, seq // 2, seq // 2)]
    layout = [(block, owner, first, count) for owner in (0, 1) for block, first, count in cuts]
    out_grad = out_gradient(pos, grads_all, gated_all, layout)
    values = row_gather(mine, half, out_grad)
    _, beside, above, *corner = values
    others = [other, *other_core(values[1:3])]
    three = [(block, owner, 0, width) for block in range(3) for owner in (0, 1)]
    pieces = [piece for pair in zip(values[:3], others, strict=True) for piece in pair]
    value_grad = value_part(after(pos, out_grad), inputs, pieces, three, (0, 1, 2), width)[0]
    others = [*others, *other_core([after(piece, value_grad) for piece in corner])]
    halves = [(0, 0, 0, half), (0, 0, half, half), (0, 1, 0, half), (0, 1, half, half)]
    value_grad, taps = value_part(
        pos,
        inputs,
        corner + others[3:],
        halves,
        (3,),
        width,
        ends=[mine, beside, above, corner[1], *others[:3], others[4]],
        taps_shape=filters.shape,
        partial=value_grad,
    )
    return (out_grad, value_grad, taps)


def toeplitz(taps, tok_rows, causal):
    filter_len = taps.shape[1]
    out_pos = lax.broadcasted_iota(jnp.int32, (tok_rows, tok_rows + filter_len), 0)
    in_pos = lax.broadcasted_iota(jnp.int32, (tok_rows, tok_rows + filter_len), 1)
    lagged = out_pos + filter_len - in_pos if causal else in_pos - out_pos
    inside = (lagged >= 0) & (lagged < filter_len)
    picked = jnp.take(taps, jnp.clip(lagged, 0, filter_len - 1), axis=1)
    return jnp.where(inside[None], picked, 0.0)


def grouped_apply(table, signal, groups):
    blocks, extent, channels = signal.shape
    split = signal.reshape(blocks, extent, groups, channels // groups)
    result = jnp.einsum("gts,bsgc->btgc", table, split, precision=highest)
    return result.reshape(blocks, table.shape[1], channels)


def taps_partial(delta_mix, mixed_ext, groups, filter_len):
    blocks, tok_rows, channels = delta_mix.shape
    left_side = delta_mix.reshape(blocks, tok_rows, groups, channels // groups)
    right_side = mixed_ext.reshape(blocks, tok_rows + filter_len, groups, channels // groups)
    products = jnp.einsum("btgc,bsgc->gts", left_side, right_side, precision=highest)
    extent = tok_rows + filter_len
    flipped = products[:, :, ::-1]
    padded = jnp.pad(flipped, ((0, 0), (0, 0), (0, tok_rows)))
    flat_rows = padded.reshape(groups, -1)[:, : tok_rows * (extent + tok_rows - 1)]
    skewed = flat_rows.reshape(groups, tok_rows, extent + tok_rows - 1)
    column_sums = jnp.sum(skewed, axis=1)
    return column_sums[:, tok_rows - 1 : tok_rows - 1 + filter_len]


def plain_local(grad_output, block_input, query_branch, key_branch, value_branch, out_weight, filters):
    filter_len = filters.shape[1]
    groups = filters.shape[0]
    tok_rows = query_branch.shape[1]
    channels = query_branch.shape[2]
    grads_all, inputs_all = (
        lax.all_gather(grad_output[0], "col", axis=0, tiled=True),
        lax.all_gather(block_input[0], "col", axis=0, tiled=True),
    )
    row_devices = lax.axis_size("row")
    sub_width = channels // row_devices
    delta_turned = lax.psum_scatter(
        lax.dot_general(
            out_weight, grads_all, (((0,), (1,)), ((), ())), preferred_element_type=jnp.float32
        ),
        "row",
        scatter_dimension=0,
        tiled=True,
    )
    queries, keys_here, values_here = (
        lax.all_to_all(query_branch[0], "row", split_axis=1, concat_axis=0, tiled=True),
        lax.all_to_all(key_branch[0], "row", split_axis=1, concat_axis=0, tiled=True),
        lax.all_to_all(value_branch[0], "row", split_axis=1, concat_axis=0, tiled=True),
    )
    delta_out = delta_turned.T
    local_groups = sub_width // (channels // groups)
    first_group = lax.axis_index("row") * local_groups
    my_taps = lax.dynamic_slice_in_dim(filters, first_group, local_groups, 0)
    mixed = keys_here.astype(jnp.float32) * values_here.astype(jnp.float32)
    mixed_blocks = mixed.reshape(row_devices, tok_rows, sub_width)
    earlier = jnp.concatenate(
        [
            jnp.zeros((1, filter_len, sub_width), jnp.float32),
            mixed_blocks[:-1, tok_rows - filter_len :],
        ],
        axis=0,
    )
    mixed_ext = jnp.concatenate([earlier, mixed_blocks], axis=1)
    conv_out = grouped_apply(toeplitz(my_taps, tok_rows, True), mixed_ext, local_groups).reshape(
        -1, sub_width
    )
    gated = (queries.astype(jnp.float32) * conv_out).astype(jnp.bfloat16)
    delta_mix = delta_out * queries.astype(jnp.float32)
    delta_blocks = delta_mix.reshape(row_devices, tok_rows, sub_width)
    later_part = jnp.concatenate(
        [delta_blocks[1:, :filter_len], jnp.zeros((1, filter_len, sub_width), jnp.float32)], axis=0
    )
    delta_ext = jnp.concatenate([delta_blocks, later_part], axis=1)
    delta_conv = grouped_apply(toeplitz(my_taps, tok_rows, False), delta_ext, local_groups).reshape(
        -1, sub_width
    )
    delta_value = (delta_conv * keys_here.astype(jnp.float32)).astype(jnp.bfloat16)
    my_terms = taps_partial(delta_blocks, mixed_ext, local_groups, filter_len)
    taps_local = lax.dynamic_update_slice_in_dim(
        jnp.zeros(filters.shape, jnp.float32), my_terms, first_group, 0
    )
    gated_all, value_all = (
        lax.all_gather(gated, "row", axis=1, tiled=True),
        lax.all_gather(delta_value, "row", axis=1, tiled=True),
    )
    out_grad = lax.dot_general(
        grads_all, gated_all, (((0,), (0,)), ((), ())), preferred_element_type=jnp.float32
    )
    value_grad = lax.dot_general(
        value_all, inputs_all, (((0,), (0,)), ((), ())), preferred_element_type=jnp.float32
    )
    out_grad, value_grad = lax.psum((out_grad, value_grad), "dp")
    taps_total = lax.psum(taps_local, ("row", "dp"))
    return (out_grad, value_grad, taps_total)


def solution(mesh):
    in_specs = (
        P("dp", "col", "row"),
        P("dp", "col", "row"),
        P("dp", "row", "col"),
        P("dp", "row", "col"),
        P("dp", "row", "col"),
        P("row", "col"),
        P("col", None),
    )
    out_specs = (P("row", "col"), P("col", "row"), P("col", None))

    def whole(*args):
        grad, filters = args[0], args[6]
        blocks_of = grad.shape[1] // mesh.shape["col"]
        width = grad.shape[2] // (mesh.shape["row"] * mesh.shape["col"])
        fits = (
            mesh.shape["row"] == 4
            and mesh.shape["col"] == 4
            and mesh.shape["dp"] == 2
            and grad.shape[0] == 2
            and blocks_of == 128
            and filters.shape[1] == 128
            and grad.shape[2] == 16 * filters.shape[0]
            and width % 512 == 0
        )
        body = local if fits else plain_local
        return jax.shard_map(body, mesh=mesh, in_specs=in_specs, out_specs=out_specs, check_vma=False)(*args)

    return whole
```

```python
import functools

import jax
import jax.numpy as jnp
from jax import lax
from jax.experimental import pallas as pl
from jax.experimental.pallas import tpu as pltpu
from jax.sharding import PartitionSpec as P

highest = lax.Precision.HIGHEST
f32, bf16 = jnp.float32, jnp.bfloat16
MIB = 1 << 20
VMEM = pl.BlockSpec(memory_space=pltpu.VMEM)
SMEM = pl.BlockSpec(memory_space=pltpu.SMEM)
ANY = pl.BlockSpec(memory_space=pl.ANY)
TILE = 256


def params():
    return pltpu.CompilerParams(vmem_limit_bytes=48 * MIB)


def cost(us):
    return pl.CostEstimate(flops=int(us * 1.15e9), bytes_accessed=0, transcendentals=0)


def split_two(x):
    hi = x.astype(bf16)
    return hi, (x - hi.astype(f32)).astype(bf16)


def turn_kernel(q_ref, k_ref, v_ref, out_ref):
    width = out_ref.shape[2]
    for j in range(out_ref.shape[0]):
        for n, src in enumerate((q_ref, k_ref, v_ref)):
            out_ref[j, n] = src[0, :, j * width : (j + 1) * width].T


def turn_branches(q, k, v, rows):
    _, toks, channels = q.shape
    return pl.pallas_call(
        turn_kernel,
        out_shape=jax.ShapeDtypeStruct((rows, 3, channels // rows, toks), bf16),
        in_specs=[VMEM] * 3,
        out_specs=VMEM,
        compiler_params=params(),
        cost_estimate=cost(3),
    )(q, k, v)


def tap_matrix(f_ref, row):
    taps = f_ref.shape[1]
    wide = jnp.broadcast_to(f_ref[pl.ds(row, 1), :], (taps, taps))
    ring = pltpu.roll(wide, 0, 1, stride=1, stride_axis=0)
    s = lax.broadcasted_iota(jnp.int32, (taps, taps), 0)
    t = lax.broadcasted_iota(jnp.int32, (taps, taps), 1)
    same = jnp.where(t >= s, ring, 0.0)
    return same, ring - same


def dot(a, b, dims=((1,), (0,))):
    return lax.dot_general(a, b, (dims, ((), ())), preferred_element_type=f32)


def forward_kernel(size, pos_ref, f_ref, parts_ref, out_ref, mh, ml, qs, gt):
    n = f_ref.shape[1]
    width, toks = gt.shape
    blocks = toks // n
    groups = width // size
    mh[:, :n] = jnp.zeros((width, n), bf16)
    ml[:, :n] = jnp.zeros((width, n), bf16)
    for j in range(blocks):
        hi, lo = split_two(parts_ref[j, 1].astype(f32) * parts_ref[j, 2].astype(f32))
        mh[:, (j + 1) * n : (j + 2) * n] = hi
        ml[:, (j + 1) * n : (j + 2) * n] = lo
        qs[:, j * n : (j + 1) * n] = parts_ref[j, 0]

    def one(g, carry):
        rows = pl.ds(pl.multiple_of(g * size, size), size)
        same, prev = tap_matrix(f_ref, pos_ref[0] * groups + g)
        table_hi, table_lo = split_two(jnp.concatenate([prev, same], axis=0))
        x_hi = jnp.concatenate([mh[rows, b * n : (b + 2) * n] for b in range(blocks)], axis=0)
        x_lo = jnp.concatenate([ml[rows, b * n : (b + 2) * n] for b in range(blocks)], axis=0)
        conv = dot(x_hi, table_hi) + dot(x_lo, table_hi) + dot(x_hi, table_lo)
        for b in range(blocks):
            gate = qs[rows, b * n : (b + 1) * n].astype(f32)
            gt[rows, b * n : (b + 1) * n] = gate * conv[b * size : (b + 1) * size]
        return carry

    lax.fori_loop(0, groups, one, 0, unroll=4)
    for b in range(blocks):
        out_ref[b * n : (b + 1) * n, :] = gt[:, b * n : (b + 1) * n].T.astype(bf16)


def forward(pos, filters, parts, size):
    rows, _, width, n = parts.shape
    toks = n * rows
    return pl.pallas_call(
        functools.partial(forward_kernel, size),
        out_shape=jax.ShapeDtypeStruct((toks, width), bf16),
        in_specs=[SMEM] + [VMEM] * 2,
        out_specs=VMEM,
        scratch_shapes=[
            pltpu.VMEM((width, toks + n), bf16),
            pltpu.VMEM((width, toks + n), bf16),
            pltpu.VMEM((width, toks), bf16),
            pltpu.VMEM((width, toks), f32),
        ],
        compiler_params=params(),
        cost_estimate=cost(0),
    )(pos, filters, parts)


def backward_kernel(size, counts, pos_ref, f_ref, parts_ref, *refs):
    n = f_ref.shape[1]
    deltas, out_ref, (dh, dl, mh, ml, qs, ks, sums) = refs[:-8], refs[-8], refs[-7:]
    width, toks = qs.shape
    blocks = toks // n
    groups = width // size
    row, col = pos_ref[0], pos_ref[1]
    zero = jnp.zeros((width, n), bf16)
    mh[:, :n] = zero
    ml[:, :n] = zero
    dh[:, toks:] = zero
    dl[:, toks:] = zero
    for j in range(blocks):
        hi, lo = split_two(parts_ref[j, 1].astype(f32) * parts_ref[j, 2].astype(f32))
        mh[:, (j + 1) * n : (j + 2) * n] = hi
        ml[:, (j + 1) * n : (j + 2) * n] = lo
        qs[:, j * n : (j + 1) * n] = parts_ref[j, 0]
        ks[:, j * n : (j + 1) * n] = parts_ref[j, 1]
    slot = 0
    for i, count in enumerate(counts):
        for m in range(count):
            place = pl.multiple_of((col ^ slot) * n, n)
            at = slice(m * n, (m + 1) * n)
            own = deltas[2 * i][at, :]
            delta = sum(jnp.where(row == j, own, deltas[2 * i + 1][j, at, :].astype(f32)) for j in range(blocks))
            hi, lo = split_two(delta.T * qs[:, pl.ds(place, n)].astype(f32))
            dh[:, pl.ds(place, n)] = hi
            dl[:, pl.ds(place, n)] = lo
            slot += 1
    s = lax.broadcasted_iota(jnp.int32, (n, n), 0)
    t = lax.broadcasted_iota(jnp.int32, (n, n), 1)

    def one(g, carry):
        rows = pl.ds(pl.multiple_of(g * size, size), size)
        same, prev = tap_matrix(f_ref, row * groups + g)
        table_hi, table_lo = split_two(jnp.concatenate([same, prev], axis=1))
        d_hi = [dh[rows, b * n : (b + 2) * n] for b in range(blocks)]
        d_lo = [dl[rows, b * n : (b + 2) * n] for b in range(blocks)]
        x_hi, x_lo = jnp.concatenate(d_hi, axis=0), jnp.concatenate(d_lo, axis=0)
        across = ((1,), (1,))
        conv = dot(x_hi, table_hi, across) + dot(x_lo, table_hi, across) + dot(x_hi, table_lo, across)
        for b in range(blocks):
            key = ks[rows, b * n : (b + 1) * n].astype(f32)
            out_ref[rows, b * n : (b + 1) * n] = (key * conv[b * size : (b + 1) * size]).astype(bf16)
        m_hi = [mh[rows, b * n : (b + 2) * n] for b in range(blocks)]
        m_lo = [ml[rows, b * n : (b + 2) * n] for b in range(blocks)]
        d_hi, d_lo = [d[:, :n] for d in d_hi], [d[:, :n] for d in d_lo]
        pairs = dot(
            jnp.concatenate(m_hi + m_lo + m_hi, axis=0),
            jnp.concatenate(d_hi + d_hi + d_lo, axis=0),
            ((0,), (0,)),
        )
        ring = jnp.where(s <= t, pairs[n:], pairs[:n])
        half = n // 2
        while half >= 8:
            ring = ring[:half] + pltpu.roll(ring[half:], n - half, 1)
            half //= 2
        sums[pl.ds(pl.multiple_of(g * 8, 8), 8), :] = ring
        return carry

    lax.fori_loop(0, groups, one, 0, unroll=4)
    total = sums[pl.ds(0, groups, stride=8), :]
    for i in range(1, 8):
        total = total + pltpu.roll(sums[pl.ds(i, groups, stride=8), :], n - i, 1)
    hi, lo = split_two(total)
    half = groups // 2
    out_ref[width:, :] = jnp.concatenate([hi[:half], hi[half:], lo[:half], lo[half:]], axis=1)


def backward(pos, filters, parts, deltas, counts, size):
    rows, _, width, n = parts.shape
    toks = n * rows
    groups = width // size
    return pl.pallas_call(
        functools.partial(backward_kernel, size, counts),
        out_shape=jax.ShapeDtypeStruct((width + groups // 2, toks), bf16),
        in_specs=[SMEM] + [VMEM] * (2 + len(deltas)),
        out_specs=VMEM,
        scratch_shapes=[pltpu.VMEM((width, toks + n), bf16)] * 4
        + [pltpu.VMEM((width, toks), bf16)] * 2
        + [pltpu.VMEM((8 * groups, n), f32)],
        compiler_params=params(),
        cost_estimate=cost(12),
    )(pos, filters, parts, *deltas)


def project_kernel(count, pos_ref, *refs):
    slots, (w_ref, own_ref, out_ref, wide, sem) = refs[:count], refs[count:]
    rows, _, width = out_ref.shape

    def fetch(j):
        return pltpu.make_async_copy(w_ref.at[:, pl.ds(j * width, width)], wide.at[j], sem.at[j])

    for j in range(rows):
        fetch(j).start()
    grads = jnp.concatenate([slot[...] for slot in slots], axis=0)
    for j in range(rows):
        fetch(j).wait()
        part = dot(grads, wide[j])
        out_ref[j] = part.astype(bf16)

        @pl.when(pos_ref[0] == j)
        def _():
            own_ref[...] = part


def project(pos, slots, weight, rows):
    depth, channels = weight.shape
    width = channels // rows
    toks = sum(slot.shape[0] for slot in slots)
    return pl.pallas_call(
        functools.partial(project_kernel, len(slots)),
        out_shape=[
            jax.ShapeDtypeStruct((toks, width), f32),
            jax.ShapeDtypeStruct((rows, toks, width), bf16),
        ],
        in_specs=[SMEM] + [VMEM] * len(slots) + [ANY],
        out_specs=[VMEM] * 2,
        scratch_shapes=[pltpu.VMEM((rows, depth, width), bf16), pltpu.SemaphoreType.DMA((rows,))],
        compiler_params=params(),
        cost_estimate=cost(8),
    )(pos, *slots, weight)


def product(left, right, buf, out_ref, sem_out, turned, places):
    tile = buf.shape[1]

    def send(i):
        at = pl.ds(pl.multiple_of(places[i], tile), tile)
        return pltpu.make_async_copy(buf.at[i % 2], out_ref.at[at, :], sem_out.at[i % 2])

    for i in range(len(places)):
        if i >= 2:
            send(i - 2).wait()
        at = slice(i * tile, (i + 1) * tile)
        buf[i % 2] = dot(left[:, at].T if turned else left[at, :], right[...])
        send(i).start()
    for i in range(max(0, len(places) - 2), len(places)):
        send(i).wait()


def run_copies(pairs, sem):
    copies = [pltpu.make_async_copy(src, dst, sem.at[i]) for i, (src, dst) in enumerate(pairs)]
    for copy in copies:
        copy.start()
    for copy in copies:
        copy.wait()


def out_kernel(n, layout, pos_ref, *refs):
    slots, pieces = refs[:8], refs[8 : 8 + len(layout)]
    out_ref, left, right, buf, sem_in, sem_out = refs[8 + len(layout) :]
    row, col = pos_ref[0], pos_ref[1]
    seq = left.shape[0] // 2
    width = right.shape[1] // 4
    pairs = []
    for i, slot in enumerate(slots):
        place = pl.multiple_of((i // 4) * seq + (col ^ (i % 4)) * n, n)
        pairs.append((slot, left.at[pl.ds(place, n), :]))
    for piece, (block, owner, first, count) in zip(pieces, layout, strict=True):
        columns = pl.ds(pl.multiple_of((row ^ block) * width, width), width)
        pairs.append((piece, right.at[pl.ds(owner * seq + first, count), columns]))
    run_copies(pairs, sem_in)
    tile = buf.shape[1]
    product(left, right, buf, out_ref, sem_out, True, [i * tile for i in range(out_ref.shape[0] // tile)])


def out_gradient(pos, slots, pieces, layout):
    n, left_width = slots[0].shape
    seq, width = pieces[0].shape
    right_width = 4 * width
    toks = 2 * seq
    return pl.pallas_call(
        functools.partial(out_kernel, n, layout),
        out_shape=jax.ShapeDtypeStruct((left_width, right_width), f32),
        in_specs=[SMEM] + [ANY] * (8 + len(pieces)),
        out_specs=ANY,
        scratch_shapes=[
            pltpu.VMEM((toks, left_width), bf16),
            pltpu.VMEM((toks, right_width), bf16),
            pltpu.VMEM((2, TILE, right_width), f32),
            pltpu.SemaphoreType.DMA((8 + len(pieces),)),
            pltpu.SemaphoreType.DMA((2,)),
        ],
        compiler_params=params(),
        cost_estimate=cost(16),
    )(pos, *slots, *pieces)


def value_kernel(n, width, which, layout, with_taps, joined, pos_ref, *refs):
    inputs, refs = refs[:8], refs[8:]
    pieces, refs = refs[: len(layout)], refs[len(layout) :]
    if with_taps:
        ends, refs = refs[:8], refs[8:]
    if joined:
        refs = refs[1:]
    out_ref, refs = refs[0], refs[1:]
    if with_taps:
        taps_ref, refs = refs[0], refs[1:]
        tails, refs = refs[-1], refs[:-1]
    left, right, buf, sem_in, sem_out = refs
    row, col = pos_ref[0], pos_ref[1]
    seq = left.shape[1] // 2
    pairs = []
    for i, slot in enumerate(inputs):
        place = pl.multiple_of((i // 4) * seq + (col ^ (i % 4)) * n, n)
        pairs.append((slot, right.at[pl.ds(place, n), :]))
    for piece, (block, owner, first, count) in zip(pieces, layout, strict=True):
        place = left.at[pl.ds(block * width + first, count), pl.ds(owner * seq, seq)]
        pairs.append((piece.at[pl.ds(0, count), :], place))
    if with_taps:
        half = tails.shape[1]
        for i, end in enumerate(ends):
            pairs.append((end.at[pl.ds(end.shape[0] - half, half), :], tails.at[i]))
    run_copies(pairs, sem_in)
    if with_taps:
        lanes = taps_ref.shape[1]
        for j in range(4):
            both = tails[j].astype(f32), tails[j + 4].astype(f32)
            cut = [[t[:, i * lanes : (i + 1) * lanes] for i in range(4)] for t in both]
            for h in range(2):
                place = pl.multiple_of((row ^ j) * 2 * half + h * half, half)
                taps_ref[pl.ds(place, half), :] = (cut[0][h] + cut[0][h + 2]) + (cut[1][h] + cut[1][h + 2])
    tile = buf.shape[1]
    places = [(row ^ j) * width + i * tile for j in which for i in range(width // tile)]
    product(left, right, buf, out_ref, sem_out, False, places)


def value_part(pos, inputs, pieces, layout, which, width, ends=(), taps_shape=None, partial=None):
    n, right_width = inputs[0].shape
    seq = pieces[0].shape[1]
    with_taps, joined = taps_shape is not None, partial is not None
    out_shape = [jax.ShapeDtypeStruct((4 * width, right_width), f32)]
    scratch = [
        pltpu.VMEM((len(which) * width, 2 * seq), bf16),
        pltpu.VMEM((2 * seq, right_width), bf16),
        pltpu.VMEM((2, TILE, right_width), f32),
        pltpu.SemaphoreType.DMA((8 + len(pieces) + len(ends),)),
        pltpu.SemaphoreType.DMA((2,)),
    ]
    operands = [pos, *inputs, *pieces, *ends]
    aliases = {}
    if with_taps:
        out_shape.append(jax.ShapeDtypeStruct(taps_shape, f32))
        scratch.append(pltpu.VMEM((8, 16, seq), bf16))
    if joined:
        aliases = {len(operands): 0}
        operands.append(partial)
    return pl.pallas_call(
        functools.partial(value_kernel, n, width, which, layout, with_taps, joined),
        out_shape=out_shape,
        in_specs=[SMEM] + [ANY] * (len(operands) - 1),
        out_specs=[ANY, VMEM][: len(out_shape)],
        scratch_shapes=scratch,
        input_output_aliases=aliases,
        compiler_params=params(),
        cost_estimate=cost(10),
    )(*operands)


near = [(0, 1), (1, 0), (2, 3), (3, 2)]
far = [(0, 2), (2, 0), (1, 3), (3, 1)]
swap = [(0, 1), (1, 0)]


def line_slots(x):
    c = lax.axis_index("col")
    first = lax.ppermute(x, "col", near)
    second = lax.ppermute(x, "col", far)
    inner = lax.ppermute(x, "col", [(1, 2), (2, 1)])
    passed = lax.ppermute(second, "col", [(2, 3), (1, 0)])
    third = jnp.where((c == 1) | (c == 2), inner, passed)
    return [x, first, second, third]


def swap_rows(x):
    return lax.all_to_all(x, "row", split_axis=0, concat_axis=0, tiled=True)


def row_gather(x, half, then=None):
    beside = lax.ppermute(x, "row", near)
    above = lax.ppermute(x, "row", far)
    if then is not None:
        beside, above, _ = lax.optimization_barrier((beside, above, then))
    return [
        x,
        beside,
        above,
        lax.ppermute(beside[:half], "row", far),
        lax.ppermute(above[half:], "row", near),
    ]


def other_core(xs):
    return [lax.ppermute(x, "dp", swap) for x in xs]


def after(pos, x):
    return lax.optimization_barrier((pos, x))[0]


def local(grad_output, block_input, query_branch, key_branch, value_branch, out_weight, filters):
    rows = lax.axis_size("row")
    toks = query_branch.shape[1]
    channels = query_branch.shape[2]
    size = channels // filters.shape[0]
    width = channels // rows
    pos = jnp.stack([lax.axis_index("row"), lax.axis_index("col"), lax.axis_index("dp")]).astype(jnp.int32)

    grads = line_slots(grad_output[0])
    turned = turn_branches(query_branch, key_branch, value_branch, rows)
    parts = swap_rows(turned)
    held = lax.optimization_barrier((block_input[0], grads[3]))
    inputs = line_slots(held[0])

    counts = (3, 1)
    deltas = []
    for chosen in (grads[:3], grads[3:]):
        own, sums = project(pos, chosen, out_weight, rows)
        pos = after(pos, own)
        if deltas:
            sums = after(sums, deltas[-1])
        deltas += [own, swap_rows(sums)]
    gated = forward(pos, filters, parts, size)
    seq = rows * toks
    gated_all = row_gather(gated, seq // 2)
    mine = backward(after(pos, (gated, inputs[1], inputs[2])), filters, parts, deltas, counts, size)
    pos, *late = lax.optimization_barrier((pos, mine, *grads, *gated_all, *inputs[:3]))
    mine, grads, gated_all, inputs = late[0], late[1:5], late[5:10], late[10:] + inputs[3:]
    half = width // 2
    inputs = inputs + other_core(inputs)
    other = other_core([mine])[0]
    gated_all = gated_all + other_core(gated_all)
    grads_all = grads + other_core(grads)
    cuts = [(0, 0, seq), (1, 0, seq), (2, 0, seq), (3, 0, seq // 2), (3, seq // 2, seq // 2)]
    layout = [(block, owner, first, count) for owner in (0, 1) for block, first, count in cuts]
    out_grad = out_gradient(pos, grads_all, gated_all, layout)
    values = row_gather(mine, half, out_grad)
    _, beside, above, *corner = values
    others = [other, *other_core(values[1:3])]
    three = [(block, owner, 0, width) for block in range(3) for owner in (0, 1)]
    pieces = [piece for pair in zip(values[:3], others, strict=True) for piece in pair]
    value_grad = value_part(after(pos, out_grad), inputs, pieces, three, (0, 1, 2), width)[0]
    others = [*others, *other_core([after(piece, value_grad) for piece in corner])]
    halves = [(0, 0, 0, half), (0, 0, half, half), (0, 1, 0, half), (0, 1, half, half)]
    value_grad, taps = value_part(
        pos,
        inputs,
        corner + others[3:],
        halves,
        (3,),
        width,
        ends=[mine, beside, above, corner[1], *others[:3], others[4]],
        taps_shape=filters.shape,
        partial=value_grad,
    )
    return (out_grad, value_grad, taps)


def toeplitz(taps, tok_rows, causal):
    filter_len = taps.shape[1]
    out_pos = lax.broadcasted_iota(jnp.int32, (tok_rows, tok_rows + filter_len), 0)
    in_pos = lax.broadcasted_iota(jnp.int32, (tok_rows, tok_rows + filter_len), 1)
    lagged = out_pos + filter_len - in_pos if causal else in_pos - out_pos
    inside = (lagged >= 0) & (lagged < filter_len)
    picked = jnp.take(taps, jnp.clip(lagged, 0, filter_len - 1), axis=1)
    return jnp.where(inside[None], picked, 0.0)


def grouped_apply(table, signal, groups):
    blocks, extent, channels = signal.shape
    split = signal.reshape(blocks, extent, groups, channels // groups)
    result = jnp.einsum("gts,bsgc->btgc", table, split, precision=highest)
    return result.reshape(blocks, table.shape[1], channels)


def taps_partial(delta_mix, mixed_ext, groups, filter_len):
    blocks, tok_rows, channels = delta_mix.shape
    left_side = delta_mix.reshape(blocks, tok_rows, groups, channels // groups)
    right_side = mixed_ext.reshape(blocks, tok_rows + filter_len, groups, channels // groups)
    products = jnp.einsum("btgc,bsgc->gts", left_side, right_side, precision=highest)
    extent = tok_rows + filter_len
    flipped = products[:, :, ::-1]
    padded = jnp.pad(flipped, ((0, 0), (0, 0), (0, tok_rows)))
    flat_rows = padded.reshape(groups, -1)[:, : tok_rows * (extent + tok_rows - 1)]
    skewed = flat_rows.reshape(groups, tok_rows, extent + tok_rows - 1)
    column_sums = jnp.sum(skewed, axis=1)
    return column_sums[:, tok_rows - 1 : tok_rows - 1 + filter_len]


def plain_local(grad_output, block_input, query_branch, key_branch, value_branch, out_weight, filters):
    filter_len = filters.shape[1]
    groups = filters.shape[0]
    tok_rows = query_branch.shape[1]
    channels = query_branch.shape[2]
    grads_all, inputs_all = (
        lax.all_gather(grad_output[0], "col", axis=0, tiled=True),
        lax.all_gather(block_input[0], "col", axis=0, tiled=True),
    )
    row_devices = lax.axis_size("row")
    sub_width = channels // row_devices
    delta_turned = lax.psum_scatter(
        lax.dot_general(
            out_weight, grads_all, (((0,), (1,)), ((), ())), preferred_element_type=jnp.float32
        ),
        "row",
        scatter_dimension=0,
        tiled=True,
    )
    queries, keys_here, values_here = (
        lax.all_to_all(query_branch[0], "row", split_axis=1, concat_axis=0, tiled=True),
        lax.all_to_all(key_branch[0], "row", split_axis=1, concat_axis=0, tiled=True),
        lax.all_to_all(value_branch[0], "row", split_axis=1, concat_axis=0, tiled=True),
    )
    delta_out = delta_turned.T
    local_groups = sub_width // (channels // groups)
    first_group = lax.axis_index("row") * local_groups
    my_taps = lax.dynamic_slice_in_dim(filters, first_group, local_groups, 0)
    mixed = keys_here.astype(jnp.float32) * values_here.astype(jnp.float32)
    mixed_blocks = mixed.reshape(row_devices, tok_rows, sub_width)
    earlier = jnp.concatenate(
        [
            jnp.zeros((1, filter_len, sub_width), jnp.float32),
            mixed_blocks[:-1, tok_rows - filter_len :],
        ],
        axis=0,
    )
    mixed_ext = jnp.concatenate([earlier, mixed_blocks], axis=1)
    conv_out = grouped_apply(toeplitz(my_taps, tok_rows, True), mixed_ext, local_groups).reshape(
        -1, sub_width
    )
    gated = (queries.astype(jnp.float32) * conv_out).astype(jnp.bfloat16)
    delta_mix = delta_out * queries.astype(jnp.float32)
    delta_blocks = delta_mix.reshape(row_devices, tok_rows, sub_width)
    later_part = jnp.concatenate(
        [delta_blocks[1:, :filter_len], jnp.zeros((1, filter_len, sub_width), jnp.float32)], axis=0
    )
    delta_ext = jnp.concatenate([delta_blocks, later_part], axis=1)
    delta_conv = grouped_apply(toeplitz(my_taps, tok_rows, False), delta_ext, local_groups).reshape(
        -1, sub_width
    )
    delta_value = (delta_conv * keys_here.astype(jnp.float32)).astype(jnp.bfloat16)
    my_terms = taps_partial(delta_blocks, mixed_ext, local_groups, filter_len)
    taps_local = lax.dynamic_update_slice_in_dim(
        jnp.zeros(filters.shape, jnp.float32), my_terms, first_group, 0
    )
    gated_all, value_all = (
        lax.all_gather(gated, "row", axis=1, tiled=True),
        lax.all_gather(delta_value, "row", axis=1, tiled=True),
    )
    out_grad = lax.dot_general(
        grads_all, gated_all, (((0,), (0,)), ((), ())), preferred_element_type=jnp.float32
    )
    value_grad = lax.dot_general(
        value_all, inputs_all, (((0,), (0,)), ((), ())), preferred_element_type=jnp.float32
    )
    out_grad, value_grad = lax.psum((out_grad, value_grad), "dp")
    taps_total = lax.psum(taps_local, ("row", "dp"))
    return (out_grad, value_grad, taps_total)


def solution(mesh):
    in_specs = (
        P("dp", "col", "row"),
        P("dp", "col", "row"),
        P("dp", "row", "col"),
        P("dp", "row", "col"),
        P("dp", "row", "col"),
        P("row", "col"),
        P("col", None),
    )
    out_specs = (P("row", "col"), P("col", "row"), P("col", None))

    def whole(*args):
        grad, filters = args[0], args[6]
        blocks_of = grad.shape[1] // mesh.shape["col"]
        width = grad.shape[2] // (mesh.shape["row"] * mesh.shape["col"])
        fits = (
            mesh.shape["row"] == 4
            and mesh.shape["col"] == 4
            and mesh.shape["dp"] == 2
            and grad.shape[0] == 2
            and blocks_of == 128
            and filters.shape[1] == 128
            and grad.shape[2] == 16 * filters.shape[0]
            and width % 512 == 0
        )
        body = local if fits else plain_local
        return jax.shard_map(body, mesh=mesh, in_specs=in_specs, out_specs=out_specs, check_vma=False)(*args)

    return whole
```

```python
import functools

import jax
import jax.numpy as jnp
from jax import lax
from jax.experimental import pallas as pl
from jax.experimental.pallas import tpu as pltpu
from jax.sharding import PartitionSpec as P

highest = lax.Precision.HIGHEST
f32, bf16 = jnp.float32, jnp.bfloat16
MIB = 1 << 20
VMEM = pl.BlockSpec(memory_space=pltpu.VMEM)
SMEM = pl.BlockSpec(memory_space=pltpu.SMEM)
ANY = pl.BlockSpec(memory_space=pl.ANY)
TILE = 256


def params():
    return pltpu.CompilerParams(vmem_limit_bytes=48 * MIB)


def cost(us):
    return pl.CostEstimate(flops=int(us * 1.15e9), bytes_accessed=0, transcendentals=0)


def split_two(x):
    hi = x.astype(bf16)
    return hi, (x - hi.astype(f32)).astype(bf16)


def turn_kernel(q_ref, k_ref, v_ref, out_ref):
    width = out_ref.shape[2]
    for j in range(out_ref.shape[0]):
        for n, src in enumerate((q_ref, k_ref, v_ref)):
            out_ref[j, n] = src[0, :, j * width : (j + 1) * width].T


def turn_branches(q, k, v, rows):
    _, toks, channels = q.shape
    return pl.pallas_call(
        turn_kernel,
        out_shape=jax.ShapeDtypeStruct((rows, 3, channels // rows, toks), bf16),
        in_specs=[VMEM] * 3,
        out_specs=VMEM,
        compiler_params=params(),
        cost_estimate=cost(3),
    )(q, k, v)


def tap_matrix(f_ref, row):
    taps = f_ref.shape[1]
    wide = jnp.broadcast_to(f_ref[pl.ds(row, 1), :], (taps, taps))
    ring = pltpu.roll(wide, 0, 1, stride=1, stride_axis=0)
    s = lax.broadcasted_iota(jnp.int32, (taps, taps), 0)
    t = lax.broadcasted_iota(jnp.int32, (taps, taps), 1)
    same = jnp.where(t >= s, ring, 0.0)
    return same, ring - same


def dot(a, b, dims=((1,), (0,))):
    return lax.dot_general(a, b, (dims, ((), ())), preferred_element_type=f32)


def forward_kernel(size, pos_ref, f_ref, parts_ref, out_ref, mh, ml, qs, gt):
    n = f_ref.shape[1]
    width, toks = gt.shape
    blocks = toks // n
    groups = width // size
    mh[:, :n] = jnp.zeros((width, n), bf16)
    ml[:, :n] = jnp.zeros((width, n), bf16)
    for j in range(blocks):
        hi, lo = split_two(parts_ref[j, 1].astype(f32) * parts_ref[j, 2].astype(f32))
        mh[:, (j + 1) * n : (j + 2) * n] = hi
        ml[:, (j + 1) * n : (j + 2) * n] = lo
        qs[:, j * n : (j + 1) * n] = parts_ref[j, 0]

    def one(g, carry):
        rows = pl.ds(pl.multiple_of(g * size, size), size)
        same, prev = tap_matrix(f_ref, pos_ref[0] * groups + g)
        table_hi, table_lo = split_two(jnp.concatenate([prev, same], axis=0))
        x_hi = jnp.concatenate([mh[rows, b * n : (b + 2) * n] for b in range(blocks)], axis=0)
        x_lo = jnp.concatenate([ml[rows, b * n : (b + 2) * n] for b in range(blocks)], axis=0)
        conv = dot(x_hi, table_hi) + dot(x_lo, table_hi) + dot(x_hi, table_lo)
        for b in range(blocks):
            gate = qs[rows, b * n : (b + 1) * n].astype(f32)
            gt[rows, b * n : (b + 1) * n] = gate * conv[b * size : (b + 1) * size]
        return carry

    lax.fori_loop(0, groups, one, 0, unroll=16)
    for b in range(blocks):
        out_ref[b * n : (b + 1) * n, :] = gt[:, b * n : (b + 1) * n].T.astype(bf16)


def forward(pos, filters, parts, size):
    rows, _, width, n = parts.shape
    toks = n * rows
    return pl.pallas_call(
        functools.partial(forward_kernel, size),
        out_shape=jax.ShapeDtypeStruct((toks, width), bf16),
        in_specs=[SMEM] + [VMEM] * 2,
        out_specs=VMEM,
        scratch_shapes=[
            pltpu.VMEM((width, toks + n), bf16),
            pltpu.VMEM((width, toks + n), bf16),
            pltpu.VMEM((width, toks), bf16),
            pltpu.VMEM((width, toks), f32),
        ],
        compiler_params=params(),
        cost_estimate=cost(0),
    )(pos, filters, parts)


def backward_kernel(size, counts, pos_ref, f_ref, parts_ref, *refs):
    n = f_ref.shape[1]
    deltas, out_ref, (dh, dl, mh, ml, qs, ks, sums) = refs[:-8], refs[-8], refs[-7:]
    width, toks = qs.shape
    blocks = toks // n
    groups = width // size
    row, col = pos_ref[0], pos_ref[1]
    zero = jnp.zeros((width, n), bf16)
    mh[:, :n] = zero
    ml[:, :n] = zero
    dh[:, toks:] = zero
    dl[:, toks:] = zero
    for j in range(blocks):
        hi, lo = split_two(parts_ref[j, 1].astype(f32) * parts_ref[j, 2].astype(f32))
        mh[:, (j + 1) * n : (j + 2) * n] = hi
        ml[:, (j + 1) * n : (j + 2) * n] = lo
        qs[:, j * n : (j + 1) * n] = parts_ref[j, 0]
        ks[:, j * n : (j + 1) * n] = parts_ref[j, 1]
    slot = 0
    for i, count in enumerate(counts):
        for m in range(count):
            place = pl.multiple_of((col ^ slot) * n, n)
            at = slice(m * n, (m + 1) * n)
            own = deltas[2 * i][at, :]
            delta = sum(jnp.where(row == j, own, deltas[2 * i + 1][j, at, :].astype(f32)) for j in range(blocks))
            hi, lo = split_two(delta.T * qs[:, pl.ds(place, n)].astype(f32))
            dh[:, pl.ds(place, n)] = hi
            dl[:, pl.ds(place, n)] = lo
            slot += 1
    s = lax.broadcasted_iota(jnp.int32, (n, n), 0)
    t = lax.broadcasted_iota(jnp.int32, (n, n), 1)

    def one(g, carry):
        rows = pl.ds(pl.multiple_of(g * size, size), size)
        same, prev = tap_matrix(f_ref, row * groups + g)
        table_hi, table_lo = split_two(jnp.concatenate([same, prev], axis=1))
        d_hi = [dh[rows, b * n : (b + 2) * n] for b in range(blocks)]
        d_lo = [dl[rows, b * n : (b + 2) * n] for b in range(blocks)]
        x_hi, x_lo = jnp.concatenate(d_hi, axis=0), jnp.concatenate(d_lo, axis=0)
        across = ((1,), (1,))
        conv = dot(x_hi, table_hi, across) + dot(x_lo, table_hi, across) + dot(x_hi, table_lo, across)
        for b in range(blocks):
            key = ks[rows, b * n : (b + 1) * n].astype(f32)
            out_ref[rows, b * n : (b + 1) * n] = (key * conv[b * size : (b + 1) * size]).astype(bf16)
        m_hi = [mh[rows, b * n : (b + 2) * n] for b in range(blocks)]
        m_lo = [ml[rows, b * n : (b + 2) * n] for b in range(blocks)]
        d_hi, d_lo = [d[:, :n] for d in d_hi], [d[:, :n] for d in d_lo]
        pairs = dot(
            jnp.concatenate(m_hi + m_lo + m_hi, axis=0),
            jnp.concatenate(d_hi + d_hi + d_lo, axis=0),
            ((0,), (0,)),
        )
        ring = jnp.where(s <= t, pairs[n:], pairs[:n])
        half = n // 2
        while half >= 8:
            ring = ring[:half] + pltpu.roll(ring[half:], n - half, 1)
            half //= 2
        sums[pl.ds(pl.multiple_of(g * 8, 8), 8), :] = ring
        return carry

    lax.fori_loop(0, groups, one, 0, unroll=16)
    total = sums[pl.ds(0, groups, stride=8), :]
    for i in range(1, 8):
        total = total + pltpu.roll(sums[pl.ds(i, groups, stride=8), :], n - i, 1)
    hi, lo = split_two(total)
    half = groups // 2
    out_ref[width:, :] = jnp.concatenate([hi[:half], hi[half:], lo[:half], lo[half:]], axis=1)


def backward(pos, filters, parts, deltas, counts, size):
    rows, _, width, n = parts.shape
    toks = n * rows
    groups = width // size
    return pl.pallas_call(
        functools.partial(backward_kernel, size, counts),
        out_shape=jax.ShapeDtypeStruct((width + groups // 2, toks), bf16),
        in_specs=[SMEM] + [VMEM] * (2 + len(deltas)),
        out_specs=VMEM,
        scratch_shapes=[pltpu.VMEM((width, toks + n), bf16)] * 4
        + [pltpu.VMEM((width, toks), bf16)] * 2
        + [pltpu.VMEM((8 * groups, n), f32)],
        compiler_params=params(),
        cost_estimate=cost(12),
    )(pos, filters, parts, *deltas)


def project_kernel(count, pos_ref, *refs):
    slots, (w_ref, own_ref, out_ref, wide, sem) = refs[:count], refs[count:]
    rows, _, width = out_ref.shape

    def fetch(j):
        return pltpu.make_async_copy(w_ref.at[:, pl.ds(j * width, width)], wide.at[j], sem.at[j])

    for j in range(rows):
        fetch(j).start()
    grads = jnp.concatenate([slot[...] for slot in slots], axis=0)
    for j in range(rows):
        fetch(j).wait()
        part = dot(grads, wide[j])
        out_ref[j] = part.astype(bf16)

        @pl.when(pos_ref[0] == j)
        def _():
            own_ref[...] = part


def project(pos, slots, weight, rows):
    depth, channels = weight.shape
    width = channels // rows
    toks = sum(slot.shape[0] for slot in slots)
    return pl.pallas_call(
        functools.partial(project_kernel, len(slots)),
        out_shape=[
            jax.ShapeDtypeStruct((toks, width), f32),
            jax.ShapeDtypeStruct((rows, toks, width), bf16),
        ],
        in_specs=[SMEM] + [VMEM] * len(slots) + [ANY],
        out_specs=[VMEM] * 2,
        scratch_shapes=[pltpu.VMEM((rows, depth, width), bf16), pltpu.SemaphoreType.DMA((rows,))],
        compiler_params=params(),
        cost_estimate=cost(8),
    )(pos, *slots, weight)


def product(left, right, buf, out_ref, sem_out, turned, places):
    tile = buf.shape[1]

    def send(i):
        at = pl.ds(pl.multiple_of(places[i], tile), tile)
        return pltpu.make_async_copy(buf.at[i % 2], out_ref.at[at, :], sem_out.at[i % 2])

    for i in range(len(places)):
        if i >= 2:
            send(i - 2).wait()
        at = slice(i * tile, (i + 1) * tile)
        buf[i % 2] = dot(left[:, at].T if turned else left[at, :], right[...])
        send(i).start()
    for i in range(max(0, len(places) - 2), len(places)):
        send(i).wait()


def run_copies(pairs, sem):
    copies = [pltpu.make_async_copy(src, dst, sem.at[i]) for i, (src, dst) in enumerate(pairs)]
    for copy in copies:
        copy.start()
    for copy in copies:
        copy.wait()


def out_kernel(n, layout, pos_ref, *refs):
    slots, pieces = refs[:8], refs[8 : 8 + len(layout)]
    out_ref, left, right, buf, sem_in, sem_out = refs[8 + len(layout) :]
    row, col = pos_ref[0], pos_ref[1]
    seq = left.shape[0] // 2
    width = right.shape[1] // 4
    pairs = []
    for i, slot in enumerate(slots):
        place = pl.multiple_of((i // 4) * seq + (col ^ (i % 4)) * n, n)
        pairs.append((slot, left.at[pl.ds(place, n), :]))
    for piece, (block, owner, first, count) in zip(pieces, layout, strict=True):
        columns = pl.ds(pl.multiple_of((row ^ block) * width, width), width)
        pairs.append((piece, right.at[pl.ds(owner * seq + first, count), columns]))
    run_copies(pairs, sem_in)
    tile = buf.shape[1]
    product(left, right, buf, out_ref, sem_out, True, [i * tile for i in range(out_ref.shape[0] // tile)])


def out_gradient(pos, slots, pieces, layout):
    n, left_width = slots[0].shape
    seq, width = pieces[0].shape
    right_width = 4 * width
    toks = 2 * seq
    return pl.pallas_call(
        functools.partial(out_kernel, n, layout),
        out_shape=jax.ShapeDtypeStruct((left_width, right_width), f32),
        in_specs=[SMEM] + [ANY] * (8 + len(pieces)),
        out_specs=ANY,
        scratch_shapes=[
            pltpu.VMEM((toks, left_width), bf16),
            pltpu.VMEM((toks, right_width), bf16),
            pltpu.VMEM((2, 2 * TILE, right_width), f32),
            pltpu.SemaphoreType.DMA((8 + len(pieces),)),
            pltpu.SemaphoreType.DMA((2,)),
        ],
        compiler_params=params(),
        cost_estimate=cost(16),
    )(pos, *slots, *pieces)


def value_kernel(n, width, which, layout, with_taps, joined, pos_ref, *refs):
    inputs, refs = refs[:8], refs[8:]
    pieces, refs = refs[: len(layout)], refs[len(layout) :]
    if with_taps:
        ends, refs = refs[:8], refs[8:]
    if joined:
        refs = refs[1:]
    out_ref, refs = refs[0], refs[1:]
    if with_taps:
        taps_ref, refs = refs[0], refs[1:]
        tails, refs = refs[-1], refs[:-1]
    left, right, buf, sem_in, sem_out = refs
    row, col = pos_ref[0], pos_ref[1]
    seq = left.shape[1] // 2
    pairs = []
    for i, slot in enumerate(inputs):
        place = pl.multiple_of((i // 4) * seq + (col ^ (i % 4)) * n, n)
        pairs.append((slot, right.at[pl.ds(place, n), :]))
    for piece, (block, owner, first, count) in zip(pieces, layout, strict=True):
        place = left.at[pl.ds(block * width + first, count), pl.ds(owner * seq, seq)]
        pairs.append((piece.at[pl.ds(0, count), :], place))
    if with_taps:
        half = tails.shape[1]
        for i, end in enumerate(ends):
            pairs.append((end.at[pl.ds(end.shape[0] - half, half), :], tails.at[i]))
    run_copies(pairs, sem_in)
    if with_taps:
        lanes = taps_ref.shape[1]
        for j in range(4):
            both = tails[j].astype(f32), tails[j + 4].astype(f32)
            cut = [[t[:, i * lanes : (i + 1) * lanes] for i in range(4)] for t in both]
            for h in range(2):
                place = pl.multiple_of((row ^ j) * 2 * half + h * half, half)
                taps_ref[pl.ds(place, half), :] = (cut[0][h] + cut[0][h + 2]) + (cut[1][h] + cut[1][h + 2])
    tile = buf.shape[1]
    places = [(row ^ j) * width + i * tile for j in which for i in range(width // tile)]
    product(left, right, buf, out_ref, sem_out, False, places)


def value_part(pos, inputs, pieces, layout, which, width, ends=(), taps_shape=None, partial=None):
    n, right_width = inputs[0].shape
    seq = pieces[0].shape[1]
    with_taps, joined = taps_shape is not None, partial is not None
    out_shape = [jax.ShapeDtypeStruct((4 * width, right_width), f32)]
    scratch = [
        pltpu.VMEM((len(which) * width, 2 * seq), bf16),
        pltpu.VMEM((2 * seq, right_width), bf16),
        pltpu.VMEM((2, TILE, right_width), f32),
        pltpu.SemaphoreType.DMA((8 + len(pieces) + len(ends),)),
        pltpu.SemaphoreType.DMA((2,)),
    ]
    operands = [pos, *inputs, *pieces, *ends]
    aliases = {}
    if with_taps:
        out_shape.append(jax.ShapeDtypeStruct(taps_shape, f32))
        scratch.append(pltpu.VMEM((8, 16, seq), bf16))
    if joined:
        aliases = {len(operands): 0}
        operands.append(partial)
    return pl.pallas_call(
        functools.partial(value_kernel, n, width, which, layout, with_taps, joined),
        out_shape=out_shape,
        in_specs=[SMEM] + [ANY] * (len(operands) - 1),
        out_specs=[ANY, VMEM][: len(out_shape)],
        scratch_shapes=scratch,
        input_output_aliases=aliases,
        compiler_params=params(),
        cost_estimate=cost(10),
    )(*operands)


near = [(0, 1), (1, 0), (2, 3), (3, 2)]
far = [(0, 2), (2, 0), (1, 3), (3, 1)]
swap = [(0, 1), (1, 0)]


def line_slots(x):
    c = lax.axis_index("col")
    first = lax.ppermute(x, "col", near)
    second = lax.ppermute(x, "col", far)
    inner = lax.ppermute(x, "col", [(1, 2), (2, 1)])
    passed = lax.ppermute(second, "col", [(2, 3), (1, 0)])
    third = jnp.where((c == 1) | (c == 2), inner, passed)
    return [x, first, second, third]


def swap_rows(x):
    return lax.all_to_all(x, "row", split_axis=0, concat_axis=0, tiled=True)


def row_gather(x, half, then=None):
    beside = lax.ppermute(x, "row", near)
    above = lax.ppermute(x, "row", far)
    if then is not None:
        beside, above, _ = lax.optimization_barrier((beside, above, then))
    return [
        x,
        beside,
        above,
        lax.ppermute(beside[:half], "row", far),
        lax.ppermute(above[half:], "row", near),
    ]


def other_core(xs):
    return [lax.ppermute(x, "dp", swap) for x in xs]


def after(pos, x):
    return lax.optimization_barrier((pos, x))[0]


def local(grad_output, block_input, query_branch, key_branch, value_branch, out_weight, filters):
    rows = lax.axis_size("row")
    toks = query_branch.shape[1]
    channels = query_branch.shape[2]
    size = channels // filters.shape[0]
    width = channels // rows
    pos = jnp.stack([lax.axis_index("row"), lax.axis_index("col"), lax.axis_index("dp")]).astype(jnp.int32)

    grads = line_slots(grad_output[0])
    turned = turn_branches(query_branch, key_branch, value_branch, rows)
    parts = swap_rows(turned)
    held = lax.optimization_barrier((block_input[0], grads[3]))
    inputs = line_slots(held[0])

    counts = (3, 1)
    deltas = []
    for chosen in (grads[:3], grads[3:]):
        own, sums = project(pos, chosen, out_weight, rows)
        pos = after(pos, own)
        if deltas:
            sums = after(sums, deltas[-1])
        deltas += [own, swap_rows(sums)]
    gated = forward(pos, filters, parts, size)
    seq = rows * toks
    gated_all = row_gather(gated, seq // 2)
    mine = backward(after(pos, (gated, inputs[1], inputs[2])), filters, parts, deltas, counts, size)
    pos, *late = lax.optimization_barrier((pos, mine, *grads, *gated_all, *inputs[:3]))
    mine, grads, gated_all, inputs = late[0], late[1:5], late[5:10], late[10:] + inputs[3:]
    half = width // 2
    inputs = inputs + other_core(inputs)
    other = other_core([mine])[0]
    gated_all = gated_all + other_core(gated_all)
    grads_all = grads + other_core(grads)
    cuts = [(0, 0, seq), (1, 0, seq), (2, 0, seq), (3, 0, seq // 2), (3, seq // 2, seq // 2)]
    layout = [(block, owner, first, count) for owner in (0, 1) for block, first, count in cuts]
    out_grad = out_gradient(pos, grads_all, gated_all, layout)
    values = row_gather(mine, half, out_grad)
    _, beside, above, *corner = values
    others = [other, *other_core(values[1:3])]
    three = [(block, owner, 0, width) for block in range(3) for owner in (0, 1)]
    pieces = [piece for pair in zip(values[:3], others, strict=True) for piece in pair]
    value_grad = value_part(after(pos, out_grad), inputs, pieces, three, (0, 1, 2), width)[0]
    others = [*others, *other_core([after(piece, value_grad) for piece in corner])]
    halves = [(0, 0, 0, half), (0, 0, half, half), (0, 1, 0, half), (0, 1, half, half)]
    value_grad, taps = value_part(
        pos,
        inputs,
        corner + others[3:],
        halves,
        (3,),
        width,
        ends=[mine, beside, above, corner[1], *others[:3], others[4]],
        taps_shape=filters.shape,
        partial=value_grad,
    )
    return (out_grad, value_grad, taps)


def toeplitz(taps, tok_rows, causal):
    filter_len = taps.shape[1]
    out_pos = lax.broadcasted_iota(jnp.int32, (tok_rows, tok_rows + filter_len), 0)
    in_pos = lax.broadcasted_iota(jnp.int32, (tok_rows, tok_rows + filter_len), 1)
    lagged = out_pos + filter_len - in_pos if causal else in_pos - out_pos
    inside = (lagged >= 0) & (lagged < filter_len)
    picked = jnp.take(taps, jnp.clip(lagged, 0, filter_len - 1), axis=1)
    return jnp.where(inside[None], picked, 0.0)


def grouped_apply(table, signal, groups):
    blocks, extent, channels = signal.shape
    split = signal.reshape(blocks, extent, groups, channels // groups)
    result = jnp.einsum("gts,bsgc->btgc", table, split, precision=highest)
    return result.reshape(blocks, table.shape[1], channels)


def taps_partial(delta_mix, mixed_ext, groups, filter_len):
    blocks, tok_rows, channels = delta_mix.shape
    left_side = delta_mix.reshape(blocks, tok_rows, groups, channels // groups)
    right_side = mixed_ext.reshape(blocks, tok_rows + filter_len, groups, channels // groups)
    products = jnp.einsum("btgc,bsgc->gts", left_side, right_side, precision=highest)
    extent = tok_rows + filter_len
    flipped = products[:, :, ::-1]
    padded = jnp.pad(flipped, ((0, 0), (0, 0), (0, tok_rows)))
    flat_rows = padded.reshape(groups, -1)[:, : tok_rows * (extent + tok_rows - 1)]
    skewed = flat_rows.reshape(groups, tok_rows, extent + tok_rows - 1)
    column_sums = jnp.sum(skewed, axis=1)
    return column_sums[:, tok_rows - 1 : tok_rows - 1 + filter_len]


def plain_local(grad_output, block_input, query_branch, key_branch, value_branch, out_weight, filters):
    filter_len = filters.shape[1]
    groups = filters.shape[0]
    tok_rows = query_branch.shape[1]
    channels = query_branch.shape[2]
    grads_all, inputs_all = (
        lax.all_gather(grad_output[0], "col", axis=0, tiled=True),
        lax.all_gather(block_input[0], "col", axis=0, tiled=True),
    )
    row_devices = lax.axis_size("row")
    sub_width = channels // row_devices
    delta_turned = lax.psum_scatter(
        lax.dot_general(
            out_weight, grads_all, (((0,), (1,)), ((), ())), preferred_element_type=jnp.float32
        ),
        "row",
        scatter_dimension=0,
        tiled=True,
    )
    queries, keys_here, values_here = (
        lax.all_to_all(query_branch[0], "row", split_axis=1, concat_axis=0, tiled=True),
        lax.all_to_all(key_branch[0], "row", split_axis=1, concat_axis=0, tiled=True),
        lax.all_to_all(value_branch[0], "row", split_axis=1, concat_axis=0, tiled=True),
    )
    delta_out = delta_turned.T
    local_groups = sub_width // (channels // groups)
    first_group = lax.axis_index("row") * local_groups
    my_taps = lax.dynamic_slice_in_dim(filters, first_group, local_groups, 0)
    mixed = keys_here.astype(jnp.float32) * values_here.astype(jnp.float32)
    mixed_blocks = mixed.reshape(row_devices, tok_rows, sub_width)
    earlier = jnp.concatenate(
        [
            jnp.zeros((1, filter_len, sub_width), jnp.float32),
            mixed_blocks[:-1, tok_rows - filter_len :],
        ],
        axis=0,
    )
    mixed_ext = jnp.concatenate([earlier, mixed_blocks], axis=1)
    conv_out = grouped_apply(toeplitz(my_taps, tok_rows, True), mixed_ext, local_groups).reshape(
        -1, sub_width
    )
    gated = (queries.astype(jnp.float32) * conv_out).astype(jnp.bfloat16)
    delta_mix = delta_out * queries.astype(jnp.float32)
    delta_blocks = delta_mix.reshape(row_devices, tok_rows, sub_width)
    later_part = jnp.concatenate(
        [delta_blocks[1:, :filter_len], jnp.zeros((1, filter_len, sub_width), jnp.float32)], axis=0
    )
    delta_ext = jnp.concatenate([delta_blocks, later_part], axis=1)
    delta_conv = grouped_apply(toeplitz(my_taps, tok_rows, False), delta_ext, local_groups).reshape(
        -1, sub_width
    )
    delta_value = (delta_conv * keys_here.astype(jnp.float32)).astype(jnp.bfloat16)
    my_terms = taps_partial(delta_blocks, mixed_ext, local_groups, filter_len)
    taps_local = lax.dynamic_update_slice_in_dim(
        jnp.zeros(filters.shape, jnp.float32), my_terms, first_group, 0
    )
    gated_all, value_all = (
        lax.all_gather(gated, "row", axis=1, tiled=True),
        lax.all_gather(delta_value, "row", axis=1, tiled=True),
    )
    out_grad = lax.dot_general(
        grads_all, gated_all, (((0,), (0,)), ((), ())), preferred_element_type=jnp.float32
    )
    value_grad = lax.dot_general(
        value_all, inputs_all, (((0,), (0,)), ((), ())), preferred_element_type=jnp.float32
    )
    out_grad, value_grad = lax.psum((out_grad, value_grad), "dp")
    taps_total = lax.psum(taps_local, ("row", "dp"))
    return (out_grad, value_grad, taps_total)


def solution(mesh):
    in_specs = (
        P("dp", "col", "row"),
        P("dp", "col", "row"),
        P("dp", "row", "col"),
        P("dp", "row", "col"),
        P("dp", "row", "col"),
        P("row", "col"),
        P("col", None),
    )
    out_specs = (P("row", "col"), P("col", "row"), P("col", None))

    def whole(*args):
        grad, filters = args[0], args[6]
        blocks_of = grad.shape[1] // mesh.shape["col"]
        width = grad.shape[2] // (mesh.shape["row"] * mesh.shape["col"])
        fits = (
            mesh.shape["row"] == 4
            and mesh.shape["col"] == 4
            and mesh.shape["dp"] == 2
            and grad.shape[0] == 2
            and blocks_of == 128
            and filters.shape[1] == 128
            and grad.shape[2] == 16 * filters.shape[0]
            and width % 512 == 0
        )
        body = local if fits else plain_local
        return jax.shard_map(body, mesh=mesh, in_specs=in_specs, out_specs=out_specs, check_vma=False)(*args)

    return whole
```

```python
import functools

import jax
import jax.numpy as jnp
from jax import lax
from jax.experimental import pallas as pl
from jax.experimental.pallas import tpu as pltpu
from jax.sharding import PartitionSpec as P

highest = lax.Precision.HIGHEST
f32, bf16 = jnp.float32, jnp.bfloat16
MIB = 1 << 20
VMEM = pl.BlockSpec(memory_space=pltpu.VMEM)
SMEM = pl.BlockSpec(memory_space=pltpu.SMEM)
ANY = pl.BlockSpec(memory_space=pl.ANY)
TILE = 256


def params():
    return pltpu.CompilerParams(vmem_limit_bytes=48 * MIB)


def cost(us):
    return pl.CostEstimate(flops=int(us * 1.15e9), bytes_accessed=0, transcendentals=0)


def split_two(x):
    hi = x.astype(bf16)
    return hi, (x - hi.astype(f32)).astype(bf16)


def turn_kernel(q_ref, k_ref, v_ref, out_ref):
    width = out_ref.shape[2]
    for j in range(out_ref.shape[0]):
        for n, src in enumerate((q_ref, k_ref, v_ref)):
            out_ref[j, n] = src[0, :, j * width : (j + 1) * width].T


def turn_branches(q, k, v, rows):
    _, toks, channels = q.shape
    return pl.pallas_call(
        turn_kernel,
        out_shape=jax.ShapeDtypeStruct((rows, 3, channels // rows, toks), bf16),
        in_specs=[VMEM] * 3,
        out_specs=VMEM,
        compiler_params=params(),
        cost_estimate=cost(3),
    )(q, k, v)


def tap_matrix(f_ref, row):
    taps = f_ref.shape[1]
    wide = jnp.broadcast_to(f_ref[pl.ds(row, 1), :], (taps, taps))
    ring = pltpu.roll(wide, 0, 1, stride=1, stride_axis=0)
    s = lax.broadcasted_iota(jnp.int32, (taps, taps), 0)
    t = lax.broadcasted_iota(jnp.int32, (taps, taps), 1)
    same = jnp.where(t >= s, ring, 0.0)
    return same, ring - same


def dot(a, b, dims=((1,), (0,))):
    return lax.dot_general(a, b, (dims, ((), ())), preferred_element_type=f32)


def forward_kernel(size, pos_ref, f_ref, parts_ref, out_ref, mh, ml, qs, gt):
    n = f_ref.shape[1]
    width, toks = gt.shape
    blocks = toks // n
    groups = width // size
    mh[:, :n] = jnp.zeros((width, n), bf16)
    ml[:, :n] = jnp.zeros((width, n), bf16)
    for j in range(blocks):
        hi, lo = split_two(parts_ref[j, 1].astype(f32) * parts_ref[j, 2].astype(f32))
        mh[:, (j + 1) * n : (j + 2) * n] = hi
        ml[:, (j + 1) * n : (j + 2) * n] = lo
        qs[:, j * n : (j + 1) * n] = parts_ref[j, 0]

    def one(g, carry):
        rows = pl.ds(pl.multiple_of(g * size, size), size)
        same, prev = tap_matrix(f_ref, pos_ref[0] * groups + g)
        table_hi, table_lo = split_two(jnp.concatenate([prev, same], axis=0))
        x_hi = jnp.concatenate([mh[rows, b * n : (b + 2) * n] for b in range(blocks)], axis=0)
        x_lo = jnp.concatenate([ml[rows, b * n : (b + 2) * n] for b in range(blocks)], axis=0)
        conv = dot(x_hi, table_hi) + dot(x_lo, table_hi) + dot(x_hi, table_lo)
        for b in range(blocks):
            gate = qs[rows, b * n : (b + 1) * n].astype(f32)
            gt[rows, b * n : (b + 1) * n] = gate * conv[b * size : (b + 1) * size]
        return carry

    lax.fori_loop(0, groups, one, 0, unroll=32)
    for b in range(blocks):
        out_ref[b * n : (b + 1) * n, :] = gt[:, b * n : (b + 1) * n].T.astype(bf16)


def forward(pos, filters, parts, size):
    rows, _, width, n = parts.shape
    toks = n * rows
    return pl.pallas_call(
        functools.partial(forward_kernel, size),
        out_shape=jax.ShapeDtypeStruct((toks, width), bf16),
        in_specs=[SMEM] + [VMEM] * 2,
        out_specs=VMEM,
        scratch_shapes=[
            pltpu.VMEM((width, toks + n), bf16),
            pltpu.VMEM((width, toks + n), bf16),
            pltpu.VMEM((width, toks), bf16),
            pltpu.VMEM((width, toks), f32),
        ],
        compiler_params=params(),
        cost_estimate=cost(0),
    )(pos, filters, parts)


def backward_kernel(size, counts, pos_ref, f_ref, parts_ref, *refs):
    n = f_ref.shape[1]
    deltas, out_ref, (dh, dl, mh, ml, qs, ks, sums) = refs[:-8], refs[-8], refs[-7:]
    width, toks = qs.shape
    blocks = toks // n
    groups = width // size
    row, col = pos_ref[0], pos_ref[1]
    zero = jnp.zeros((width, n), bf16)
    mh[:, :n] = zero
    ml[:, :n] = zero
    dh[:, toks:] = zero
    dl[:, toks:] = zero
    for j in range(blocks):
        hi, lo = split_two(parts_ref[j, 1].astype(f32) * parts_ref[j, 2].astype(f32))
        mh[:, (j + 1) * n : (j + 2) * n] = hi
        ml[:, (j + 1) * n : (j + 2) * n] = lo
        qs[:, j * n : (j + 1) * n] = parts_ref[j, 0]
        ks[:, j * n : (j + 1) * n] = parts_ref[j, 1]
    slot = 0
    for i, count in enumerate(counts):
        for m in range(count):
            place = pl.multiple_of((col ^ slot) * n, n)
            at = slice(m * n, (m + 1) * n)
            own = deltas[2 * i][at, :]
            delta = sum(jnp.where(row == j, own, deltas[2 * i + 1][j, at, :].astype(f32)) for j in range(blocks))
            hi, lo = split_two(delta.T * qs[:, pl.ds(place, n)].astype(f32))
            dh[:, pl.ds(place, n)] = hi
            dl[:, pl.ds(place, n)] = lo
            slot += 1
    s = lax.broadcasted_iota(jnp.int32, (n, n), 0)
    t = lax.broadcasted_iota(jnp.int32, (n, n), 1)

    def one(g, carry):
        rows = pl.ds(pl.multiple_of(g * size, size), size)
        same, prev = tap_matrix(f_ref, row * groups + g)
        table_hi, table_lo = split_two(jnp.concatenate([same, prev], axis=1))
        d_hi = [dh[rows, b * n : (b + 2) * n] for b in range(blocks)]
        d_lo = [dl[rows, b * n : (b + 2) * n] for b in range(blocks)]
        x_hi, x_lo = jnp.concatenate(d_hi, axis=0), jnp.concatenate(d_lo, axis=0)
        across = ((1,), (1,))
        conv = dot(x_hi, table_hi, across) + dot(x_lo, table_hi, across) + dot(x_hi, table_lo, across)
        for b in range(blocks):
            key = ks[rows, b * n : (b + 1) * n].astype(f32)
            out_ref[rows, b * n : (b + 1) * n] = (key * conv[b * size : (b + 1) * size]).astype(bf16)
        m_hi = [mh[rows, b * n : (b + 2) * n] for b in range(blocks)]
        m_lo = [ml[rows, b * n : (b + 2) * n] for b in range(blocks)]
        d_hi, d_lo = [d[:, :n] for d in d_hi], [d[:, :n] for d in d_lo]
        pairs = dot(
            jnp.concatenate(m_hi + m_lo + m_hi, axis=0),
            jnp.concatenate(d_hi + d_hi + d_lo, axis=0),
            ((0,), (0,)),
        )
        ring = jnp.where(s <= t, pairs[n:], pairs[:n])
        half = n // 2
        while half >= 8:
            ring = ring[:half] + pltpu.roll(ring[half:], n - half, 1)
            half //= 2
        sums[pl.ds(pl.multiple_of(g * 8, 8), 8), :] = ring
        return carry

    lax.fori_loop(0, groups, one, 0, unroll=32)
    total = sums[pl.ds(0, groups, stride=8), :]
    for i in range(1, 8):
        total = total + pltpu.roll(sums[pl.ds(i, groups, stride=8), :], n - i, 1)
    hi, lo = split_two(total)
    half = groups // 2
    out_ref[width:, :] = jnp.concatenate([hi[:half], hi[half:], lo[:half], lo[half:]], axis=1)


def backward(pos, filters, parts, deltas, counts, size):
    rows, _, width, n = parts.shape
    toks = n * rows
    groups = width // size
    return pl.pallas_call(
        functools.partial(backward_kernel, size, counts),
        out_shape=jax.ShapeDtypeStruct((width + groups // 2, toks), bf16),
        in_specs=[SMEM] + [VMEM] * (2 + len(deltas)),
        out_specs=VMEM,
        scratch_shapes=[pltpu.VMEM((width, toks + n), bf16)] * 4
        + [pltpu.VMEM((width, toks), bf16)] * 2
        + [pltpu.VMEM((8 * groups, n), f32)],
        compiler_params=params(),
        cost_estimate=cost(12),
    )(pos, filters, parts, *deltas)


def project_kernel(count, pos_ref, *refs):
    slots, (w_ref, own_ref, out_ref, wide, sem) = refs[:count], refs[count:]
    rows, _, width = out_ref.shape

    def fetch(j):
        return pltpu.make_async_copy(w_ref.at[:, pl.ds(j * width, width)], wide.at[j], sem.at[j])

    for j in range(rows):
        fetch(j).start()
    grads = jnp.concatenate([slot[...] for slot in slots], axis=0)
    for j in range(rows):
        fetch(j).wait()
        part = dot(grads, wide[j])
        out_ref[j] = part.astype(bf16)

        @pl.when(pos_ref[0] == j)
        def _():
            own_ref[...] = part


def project(pos, slots, weight, rows):
    depth, channels = weight.shape
    width = channels // rows
    toks = sum(slot.shape[0] for slot in slots)
    return pl.pallas_call(
        functools.partial(project_kernel, len(slots)),
        out_shape=[
            jax.ShapeDtypeStruct((toks, width), f32),
            jax.ShapeDtypeStruct((rows, toks, width), bf16),
        ],
        in_specs=[SMEM] + [VMEM] * len(slots) + [ANY],
        out_specs=[VMEM] * 2,
        scratch_shapes=[pltpu.VMEM((rows, depth, width), bf16), pltpu.SemaphoreType.DMA((rows,))],
        compiler_params=params(),
        cost_estimate=cost(8),
    )(pos, *slots, weight)


def product(left, right, buf, out_ref, sem_out, turned, places):
    tile = buf.shape[1]

    def send(i):
        at = pl.ds(pl.multiple_of(places[i], tile), tile)
        return pltpu.make_async_copy(buf.at[i % 2], out_ref.at[at, :], sem_out.at[i % 2])

    for i in range(len(places)):
        if i >= 2:
            send(i - 2).wait()
        at = slice(i * tile, (i + 1) * tile)
        buf[i % 2] = dot(left[:, at].T if turned else left[at, :], right[...])
        send(i).start()
    for i in range(max(0, len(places) - 2), len(places)):
        send(i).wait()


def run_copies(pairs, sem):
    copies = [pltpu.make_async_copy(src, dst, sem.at[i]) for i, (src, dst) in enumerate(pairs)]
    for copy in copies:
        copy.start()
    for copy in copies:
        copy.wait()


def out_kernel(n, layout, pos_ref, *refs):
    slots, pieces = refs[:8], refs[8 : 8 + len(layout)]
    out_ref, left, right, buf, sem_in, sem_out = refs[8 + len(layout) :]
    row, col = pos_ref[0], pos_ref[1]
    seq = left.shape[0] // 2
    width = right.shape[1] // 4
    pairs = []
    for i, slot in enumerate(slots):
        place = pl.multiple_of((i // 4) * seq + (col ^ (i % 4)) * n, n)
        pairs.append((slot, left.at[pl.ds(place, n), :]))
    for piece, (block, owner, first, count) in zip(pieces, layout, strict=True):
        columns = pl.ds(pl.multiple_of((row ^ block) * width, width), width)
        pairs.append((piece, right.at[pl.ds(owner * seq + first, count), columns]))
    run_copies(pairs, sem_in)
    tile = buf.shape[1]
    product(left, right, buf, out_ref, sem_out, True, [i * tile for i in range(out_ref.shape[0] // tile)])


def out_gradient(pos, slots, pieces, layout):
    n, left_width = slots[0].shape
    seq, width = pieces[0].shape
    right_width = 4 * width
    toks = 2 * seq
    return pl.pallas_call(
        functools.partial(out_kernel, n, layout),
        out_shape=jax.ShapeDtypeStruct((left_width, right_width), f32),
        in_specs=[SMEM] + [ANY] * (8 + len(pieces)),
        out_specs=ANY,
        scratch_shapes=[
            pltpu.VMEM((toks, left_width), bf16),
            pltpu.VMEM((toks, right_width), bf16),
            pltpu.VMEM((2, 2 * TILE, right_width), f32),
            pltpu.SemaphoreType.DMA((8 + len(pieces),)),
            pltpu.SemaphoreType.DMA((2,)),
        ],
        compiler_params=params(),
        cost_estimate=cost(16),
    )(pos, *slots, *pieces)


def value_kernel(n, width, which, layout, with_taps, joined, pos_ref, *refs):
    inputs, refs = refs[:8], refs[8:]
    pieces, refs = refs[: len(layout)], refs[len(layout) :]
    if with_taps:
        ends, refs = refs[:8], refs[8:]
    if joined:
        refs = refs[1:]
    out_ref, refs = refs[0], refs[1:]
    if with_taps:
        taps_ref, refs = refs[0], refs[1:]
        tails, refs = refs[-1], refs[:-1]
    left, right, buf, sem_in, sem_out = refs
    row, col = pos_ref[0], pos_ref[1]
    seq = left.shape[1] // 2
    pairs = []
    for i, slot in enumerate(inputs):
        place = pl.multiple_of((i // 4) * seq + (col ^ (i % 4)) * n, n)
        pairs.append((slot, right.at[pl.ds(place, n), :]))
    for piece, (block, owner, first, count) in zip(pieces, layout, strict=True):
        place = left.at[pl.ds(block * width + first, count), pl.ds(owner * seq, seq)]
        pairs.append((piece.at[pl.ds(0, count), :], place))
    if with_taps:
        half = tails.shape[1]
        for i, end in enumerate(ends):
            pairs.append((end.at[pl.ds(end.shape[0] - half, half), :], tails.at[i]))
    run_copies(pairs, sem_in)
    if with_taps:
        lanes = taps_ref.shape[1]
        for j in range(4):
            both = tails[j].astype(f32), tails[j + 4].astype(f32)
            cut = [[t[:, i * lanes : (i + 1) * lanes] for i in range(4)] for t in both]
            for h in range(2):
                place = pl.multiple_of((row ^ j) * 2 * half + h * half, half)
                taps_ref[pl.ds(place, half), :] = (cut[0][h] + cut[0][h + 2]) + (cut[1][h] + cut[1][h + 2])
    tile = buf.shape[1]
    places = [(row ^ j) * width + i * tile for j in which for i in range(width // tile)]
    product(left, right, buf, out_ref, sem_out, False, places)


def value_part(pos, inputs, pieces, layout, which, width, ends=(), taps_shape=None, partial=None):
    n, right_width = inputs[0].shape
    seq = pieces[0].shape[1]
    with_taps, joined = taps_shape is not None, partial is not None
    out_shape = [jax.ShapeDtypeStruct((4 * width, right_width), f32)]
    scratch = [
        pltpu.VMEM((len(which) * width, 2 * seq), bf16),
        pltpu.VMEM((2 * seq, right_width), bf16),
        pltpu.VMEM((2, TILE, right_width), f32),
        pltpu.SemaphoreType.DMA((8 + len(pieces) + len(ends),)),
        pltpu.SemaphoreType.DMA((2,)),
    ]
    operands = [pos, *inputs, *pieces, *ends]
    aliases = {}
    if with_taps:
        out_shape.append(jax.ShapeDtypeStruct(taps_shape, f32))
        scratch.append(pltpu.VMEM((8, 16, seq), bf16))
    if joined:
        aliases = {len(operands): 0}
        operands.append(partial)
    return pl.pallas_call(
        functools.partial(value_kernel, n, width, which, layout, with_taps, joined),
        out_shape=out_shape,
        in_specs=[SMEM] + [ANY] * (len(operands) - 1),
        out_specs=[ANY, VMEM][: len(out_shape)],
        scratch_shapes=scratch,
        input_output_aliases=aliases,
        compiler_params=params(),
        cost_estimate=cost(10),
    )(*operands)


near = [(0, 1), (1, 0), (2, 3), (3, 2)]
far = [(0, 2), (2, 0), (1, 3), (3, 1)]
swap = [(0, 1), (1, 0)]


def line_slots(x):
    c = lax.axis_index("col")
    first = lax.ppermute(x, "col", near)
    second = lax.ppermute(x, "col", far)
    inner = lax.ppermute(x, "col", [(1, 2), (2, 1)])
    passed = lax.ppermute(second, "col", [(2, 3), (1, 0)])
    third = jnp.where((c == 1) | (c == 2), inner, passed)
    return [x, first, second, third]


def swap_rows(x):
    return lax.all_to_all(x, "row", split_axis=0, concat_axis=0, tiled=True)


def row_gather(x, half, then=None):
    beside = lax.ppermute(x, "row", near)
    above = lax.ppermute(x, "row", far)
    if then is not None:
        beside, above, _ = lax.optimization_barrier((beside, above, then))
    return [
        x,
        beside,
        above,
        lax.ppermute(beside[:half], "row", far),
        lax.ppermute(above[half:], "row", near),
    ]


def other_core(xs):
    return [lax.ppermute(x, "dp", swap) for x in xs]


def after(pos, x):
    return lax.optimization_barrier((pos, x))[0]


def local(grad_output, block_input, query_branch, key_branch, value_branch, out_weight, filters):
    rows = lax.axis_size("row")
    toks = query_branch.shape[1]
    channels = query_branch.shape[2]
    size = channels // filters.shape[0]
    width = channels // rows
    pos = jnp.stack([lax.axis_index("row"), lax.axis_index("col"), lax.axis_index("dp")]).astype(jnp.int32)

    grads = line_slots(grad_output[0])
    turned = turn_branches(query_branch, key_branch, value_branch, rows)
    parts = swap_rows(turned)
    held = lax.optimization_barrier((block_input[0], grads[3]))
    inputs = line_slots(held[0])

    counts = (3, 1)
    deltas = []
    for chosen in (grads[:3], grads[3:]):
        own, sums = project(pos, chosen, out_weight, rows)
        pos = after(pos, own)
        if deltas:
            sums = after(sums, deltas[-1])
        deltas += [own, swap_rows(sums)]
    gated = forward(pos, filters, parts, size)
    seq = rows * toks
    gated_all = row_gather(gated, seq // 2)
    mine = backward(after(pos, (gated, inputs[1], inputs[2])), filters, parts, deltas, counts, size)
    pos, *late = lax.optimization_barrier((pos, mine, *grads, *gated_all, *inputs[:3]))
    mine, grads, gated_all, inputs = late[0], late[1:5], late[5:10], late[10:] + inputs[3:]
    half = width // 2
    inputs = inputs + other_core(inputs)
    other = other_core([mine])[0]
    gated_all = gated_all + other_core(gated_all)
    grads_all = grads + other_core(grads)
    cuts = [(0, 0, seq), (1, 0, seq), (2, 0, seq), (3, 0, seq // 2), (3, seq // 2, seq // 2)]
    layout = [(block, owner, first, count) for owner in (0, 1) for block, first, count in cuts]
    out_grad = out_gradient(pos, grads_all, gated_all, layout)
    values = row_gather(mine, half, out_grad)
    _, beside, above, *corner = values
    others = [other, *other_core(values[1:3])]
    three = [(block, owner, 0, width) for block in range(3) for owner in (0, 1)]
    pieces = [piece for pair in zip(values[:3], others, strict=True) for piece in pair]
    value_grad = value_part(after(pos, out_grad), inputs, pieces, three, (0, 1, 2), width)[0]
    others = [*others, *other_core([after(piece, value_grad) for piece in corner])]
    halves = [(0, 0, 0, half), (0, 0, half, half), (0, 1, 0, half), (0, 1, half, half)]
    value_grad, taps = value_part(
        pos,
        inputs,
        corner + others[3:],
        halves,
        (3,),
        width,
        ends=[mine, beside, above, corner[1], *others[:3], others[4]],
        taps_shape=filters.shape,
        partial=value_grad,
    )
    return (out_grad, value_grad, taps)


def toeplitz(taps, tok_rows, causal):
    filter_len = taps.shape[1]
    out_pos = lax.broadcasted_iota(jnp.int32, (tok_rows, tok_rows + filter_len), 0)
    in_pos = lax.broadcasted_iota(jnp.int32, (tok_rows, tok_rows + filter_len), 1)
    lagged = out_pos + filter_len - in_pos if causal else in_pos - out_pos
    inside = (lagged >= 0) & (lagged < filter_len)
    picked = jnp.take(taps, jnp.clip(lagged, 0, filter_len - 1), axis=1)
    return jnp.where(inside[None], picked, 0.0)


def grouped_apply(table, signal, groups):
    blocks, extent, channels = signal.shape
    split = signal.reshape(blocks, extent, groups, channels // groups)
    result = jnp.einsum("gts,bsgc->btgc", table, split, precision=highest)
    return result.reshape(blocks, table.shape[1], channels)


def taps_partial(delta_mix, mixed_ext, groups, filter_len):
    blocks, tok_rows, channels = delta_mix.shape
    left_side = delta_mix.reshape(blocks, tok_rows, groups, channels // groups)
    right_side = mixed_ext.reshape(blocks, tok_rows + filter_len, groups, channels // groups)
    products = jnp.einsum("btgc,bsgc->gts", left_side, right_side, precision=highest)
    extent = tok_rows + filter_len
    flipped = products[:, :, ::-1]
    padded = jnp.pad(flipped, ((0, 0), (0, 0), (0, tok_rows)))
    flat_rows = padded.reshape(groups, -1)[:, : tok_rows * (extent + tok_rows - 1)]
    skewed = flat_rows.reshape(groups, tok_rows, extent + tok_rows - 1)
    column_sums = jnp.sum(skewed, axis=1)
    return column_sums[:, tok_rows - 1 : tok_rows - 1 + filter_len]


def plain_local(grad_output, block_input, query_branch, key_branch, value_branch, out_weight, filters):
    filter_len = filters.shape[1]
    groups = filters.shape[0]
    tok_rows = query_branch.shape[1]
    channels = query_branch.shape[2]
    grads_all, inputs_all = (
        lax.all_gather(grad_output[0], "col", axis=0, tiled=True),
        lax.all_gather(block_input[0], "col", axis=0, tiled=True),
    )
    row_devices = lax.axis_size("row")
    sub_width = channels // row_devices
    delta_turned = lax.psum_scatter(
        lax.dot_general(
            out_weight, grads_all, (((0,), (1,)), ((), ())), preferred_element_type=jnp.float32
        ),
        "row",
        scatter_dimension=0,
        tiled=True,
    )
    queries, keys_here, values_here = (
        lax.all_to_all(query_branch[0], "row", split_axis=1, concat_axis=0, tiled=True),
        lax.all_to_all(key_branch[0], "row", split_axis=1, concat_axis=0, tiled=True),
        lax.all_to_all(value_branch[0], "row", split_axis=1, concat_axis=0, tiled=True),
    )
    delta_out = delta_turned.T
    local_groups = sub_width // (channels // groups)
    first_group = lax.axis_index("row") * local_groups
    my_taps = lax.dynamic_slice_in_dim(filters, first_group, local_groups, 0)
    mixed = keys_here.astype(jnp.float32) * values_here.astype(jnp.float32)
    mixed_blocks = mixed.reshape(row_devices, tok_rows, sub_width)
    earlier = jnp.concatenate(
        [
            jnp.zeros((1, filter_len, sub_width), jnp.float32),
            mixed_blocks[:-1, tok_rows - filter_len :],
        ],
        axis=0,
    )
    mixed_ext = jnp.concatenate([earlier, mixed_blocks], axis=1)
    conv_out = grouped_apply(toeplitz(my_taps, tok_rows, True), mixed_ext, local_groups).reshape(
        -1, sub_width
    )
    gated = (queries.astype(jnp.float32) * conv_out).astype(jnp.bfloat16)
    delta_mix = delta_out * queries.astype(jnp.float32)
    delta_blocks = delta_mix.reshape(row_devices, tok_rows, sub_width)
    later_part = jnp.concatenate(
        [delta_blocks[1:, :filter_len], jnp.zeros((1, filter_len, sub_width), jnp.float32)], axis=0
    )
    delta_ext = jnp.concatenate([delta_blocks, later_part], axis=1)
    delta_conv = grouped_apply(toeplitz(my_taps, tok_rows, False), delta_ext, local_groups).reshape(
        -1, sub_width
    )
    delta_value = (delta_conv * keys_here.astype(jnp.float32)).astype(jnp.bfloat16)
    my_terms = taps_partial(delta_blocks, mixed_ext, local_groups, filter_len)
    taps_local = lax.dynamic_update_slice_in_dim(
        jnp.zeros(filters.shape, jnp.float32), my_terms, first_group, 0
    )
    gated_all, value_all = (
        lax.all_gather(gated, "row", axis=1, tiled=True),
        lax.all_gather(delta_value, "row", axis=1, tiled=True),
    )
    out_grad = lax.dot_general(
        grads_all, gated_all, (((0,), (0,)), ((), ())), preferred_element_type=jnp.float32
    )
    value_grad = lax.dot_general(
        value_all, inputs_all, (((0,), (0,)), ((), ())), preferred_element_type=jnp.float32
    )
    out_grad, value_grad = lax.psum((out_grad, value_grad), "dp")
    taps_total = lax.psum(taps_local, ("row", "dp"))
    return (out_grad, value_grad, taps_total)


def solution(mesh):
    in_specs = (
        P("dp", "col", "row"),
        P("dp", "col", "row"),
        P("dp", "row", "col"),
        P("dp", "row", "col"),
        P("dp", "row", "col"),
        P("row", "col"),
        P("col", None),
    )
    out_specs = (P("row", "col"), P("col", "row"), P("col", None))

    def whole(*args):
        grad, filters = args[0], args[6]
        blocks_of = grad.shape[1] // mesh.shape["col"]
        width = grad.shape[2] // (mesh.shape["row"] * mesh.shape["col"])
        fits = (
            mesh.shape["row"] == 4
            and mesh.shape["col"] == 4
            and mesh.shape["dp"] == 2
            and grad.shape[0] == 2
            and blocks_of == 128
            and filters.shape[1] == 128
            and grad.shape[2] == 16 * filters.shape[0]
            and width % 512 == 0
        )
        body = local if fits else plain_local
        return jax.shard_map(body, mesh=mesh, in_specs=in_specs, out_specs=out_specs, check_vma=False)(*args)

    return whole
```
